32 devices in a mesh: section: 1, expert: 32 (over z, y, x, core).
Axes of the slice: x: 2, y: 2, z: 4, core: 2. Of those that a mesh axis runs over, the one named last changes fastest.
Arguments:
- feat_saved: bfloat16 [1, 2, 4096, 1024], P('section', None, 'expert'), may hold values from -6 to 6
- out_grad: bfloat16 [2, 4096, 1024], P(None, 'expert'), may hold values from -6 to 6
- lengths: int32 [2, 32], P(None, 'expert'), may hold values from 32 to 128, as said below
- expert_ids: int32 [1, 2, 4096], P('section', None, 'expert'), may hold values from 0 to 31, as said below
- slot_ids: int32 [1, 2, 4096], P('section', None, 'expert'), may hold values from 0 to 5, as said below
- expert_preact: bfloat16 [1, 2, 6144, 640], P('section', None, 'expert'), may hold values from -6 to 6
- conv_weight: bfloat16 [1, 32, 1024], P('section'), may hold values from -0.5 to 0.5
- norm_gain: bfloat16 [1, 1024], P('section'), may hold values from 0.5 to 1.5
- centroids: bfloat16 [1, 32, 1024], P('section'), may hold values from -0.375 to 0.375
- w_in: bfloat16 [1, 32, 1024, 640], P('section', 'expert'), may hold values from -0.1875 to 0.1875
- w_out: bfloat16 [1, 32, 640, 1024], P('section', 'expert'), may hold values from -0.25 to 0.25
Outputs:
- section_grads: bfloat16 [1, 2, 4096, 1024], P('section', None, 'expert')
The draws below stay inside these ranges and needn't reach their ends.
Inputs may be any that keep to these rules, and one draw needn't show every extreme that they name: `expert_ids`: in every block and micro-batch, the 128 frames of one utterance name each expert at most 6 times, and one expert is named exactly 6 times by the frames of every utterance. `slot_ids`: within one utterance's frames of one block and micro-batch, the frames that name the same expert hold the slots 0, 1, ... up to their count less one, each once. `lengths`: in every micro-batch at least one utterance has all 128 frames.
All inputs are finite; a program needn't handle non-finite values.
Results may differ from the reference program's by a relative error of at most 0.02.
Values may be sent and summed in bfloat16 or wider, within the bound.
A program may use at most 64 MiB of HBM per device.

```python
import math
import jax
import jax.numpy as jnp
from jax import lax

D = 1024
HID = 640
KER = 32
FRAMES_DEV = 128
MICRO = 2
SECTIONS = 1
EXPERTS = 32
UTTS = 32
FRAMES = 4096
CAP = 6
SLOTS = 192


def routing_tables(key):
    candidates = EXPERTS * CAP
    hot_expert = jax.random.randint(jax.random.fold_in(key, 11), (SECTIONS, MICRO, 1, 1, 1), 0, EXPERTS)
    table_shape = (SECTIONS, MICRO, EXPERTS, EXPERTS, 1)
    strides = jax.random.randint(jax.random.fold_in(key, 12), table_shape, 3, 13)
    offsets = jax.random.randint(jax.random.fold_in(key, 13), table_shape, 0, 4)
    expert_idx = jnp.arange(EXPERTS).astype(jnp.int32).reshape(1, 1, 1, EXPERTS, 1)
    slot_idx = jnp.arange(CAP).astype(jnp.int32).reshape(1, 1, 1, 1, CAP)
    is_hot = expert_idx == hot_expert
    strides = jnp.where(is_hot, 1, strides)
    offsets = jnp.where(is_hot, 0, offsets)
    order_key = slot_idx * strides + offsets
    rank_val = (expert_idx - hot_expert) % EXPERTS * CAP + slot_idx
    scores = (order_key * candidates + rank_val).reshape(SECTIONS, MICRO, EXPERTS, candidates)
    chosen_neg, chosen = lax.top_k(-scores, FRAMES_DEV)
    chosen_expert = chosen // CAP
    chosen_slot = chosen % CAP
    shuffle_raw = jax.random.randint(jax.random.fold_in(key, 14), (SECTIONS, MICRO, EXPERTS, FRAMES_DEV), 0, 2 ** 20) * FRAMES_DEV + jnp.arange(FRAMES_DEV).astype(jnp.int32)
    shuffle_val, shuffle = lax.top_k(shuffle_raw, FRAMES_DEV)
    routed = jnp.take_along_axis(chosen_expert, shuffle, axis=3).reshape(SECTIONS, MICRO, EXPERTS * FRAMES_DEV)
    slot_rows = jnp.take_along_axis(chosen_slot, shuffle, axis=3).reshape(SECTIONS, MICRO, EXPERTS * FRAMES_DEV)
    return (routed.astype(jnp.int32), slot_rows.astype(jnp.int32))


def draw_expert_ids(key, part):
    return routing_tables(key)[0]


def draw_slot_ids(key, part):
    return routing_tables(key)[1]


def draw_lengths(key, part):
    base_len = jax.random.randint(jax.random.fold_in(key, 21), (MICRO, UTTS), FRAMES_DEV // 4, FRAMES_DEV + 1)
    full_utt = jax.random.randint(jax.random.fold_in(key, 22), (MICRO, 1), 0, UTTS)
    utt_idx = jnp.arange(UTTS).astype(jnp.int32)[None, :]
    return jnp.where(utt_idx == full_utt, FRAMES_DEV, base_len).astype(jnp.int32)


def levels(rng, shape, shards, least, top_value):
    def one(axis_at, parts):
        heights = jax.random.uniform(jax.random.fold_in(jax.random.fold_in(rng, 6), axis_at), (parts,), jnp.float32, least / len(shards), top_value / len(shards))
        return jnp.repeat(jnp.exp(heights), shape[axis_at] // parts).reshape((-1,) + (1,) * (len(shape) - axis_at - 1))

    gain = one(*shards[0])
    for cut in shards[1:]:
        gain = gain * one(*cut)
    return gain


def noise(stream_key, extent, width, limit, cuts=(), held_as=jnp.bfloat16):
    level = levels(stream_key, extent, cuts, -0.22, 0.18) if cuts else 1.0
    entries = jax.random.normal(stream_key, extent, jnp.float32) * width * level
    return jnp.minimum(jnp.maximum(entries, -limit), limit).astype(held_as)


def setup_inputs(seed: int = 0) -> dict:
    splits = jax.random.split(jax.random.key(seed), 12)
    feat_saved = noise(splits[0], (SECTIONS, MICRO, FRAMES, D), 1.0, 6.0, ((2, 32),))
    out_grad = noise(splits[1], (MICRO, FRAMES, D), 1.0, 6.0, ((1, 32),))
    lengths = draw_lengths(jax.random.fold_in(splits[11], 71), 0)
    expert_ids = draw_expert_ids(jax.random.fold_in(splits[11], 71), 0)
    slot_ids = draw_slot_ids(jax.random.fold_in(splits[11], 71), 0)
    expert_preact = noise(splits[5], (SECTIONS, MICRO, EXPERTS * SLOTS, HID), 1.0, 6.0, ((2, 32),))
    conv_weight = noise(splits[6], (SECTIONS, KER, D), (4 * KER) ** -0.5, 0.5)
    norm_gain = jnp.clip(1.0 + 0.1 * jax.random.normal(splits[7], (SECTIONS, D), jnp.float32), 0.5, 1.5).astype(jnp.bfloat16)
    centroids = noise(splits[8], (SECTIONS, EXPERTS, D), (D // 4) ** -0.5, 0.375)
    w_in = noise(splits[9], (SECTIONS, EXPERTS, D, HID), D ** -0.5, 0.1875, ((1, 32),))
    w_out = noise(splits[10], (SECTIONS, EXPERTS, HID, D), HID ** -0.5, 0.25, ((1, 32),))
    return {"feat_saved": feat_saved, "out_grad": out_grad, "lengths": lengths, "expert_ids": expert_ids, "slot_ids": slot_ids, "expert_preact": expert_preact, "conv_weight": conv_weight, "norm_gain": norm_gain, "centroids": centroids, "w_in": w_in, "w_out": w_out}


def time_conv(values, kernel, low_pad):
    tap_count = kernel.shape[0]
    frames = values.shape[-2]
    widths = [(0, 0)] * (values.ndim - 2) + [(low_pad, tap_count - 1 - low_pad), (0, 0)]
    padded = jnp.pad(values, widths)
    summed = jnp.zeros_like(values)
    for tap_idx in range(tap_count):
        summed = summed + kernel[tap_idx] * lax.slice_in_dim(padded, tap_idx, tap_idx + frames, axis=values.ndim - 2)
    return summed

def gelu_parts(preact):
    act_val = preact.astype(jnp.float32)
    cdf_val = 0.5 * (1.0 + jax.scipy.special.erf(act_val * (1.0 / math.sqrt(2.0))))
    gelu_val = act_val * cdf_val
    gelu_slope = cdf_val + act_val * jnp.exp(-0.5 * act_val * act_val) * (1.0 / math.sqrt(2.0 * math.pi))
    return (gelu_val, gelu_slope)

def expert_back(operands):
    slot_rows, preact, weight_in, weight_out = operands
    hidden_grad = lax.dot_general(slot_rows, weight_out, (((1,), (1,)), ((), ())), preferred_element_type=jnp.float32)
    gelu_val, gelu_slope = gelu_parts(preact)
    gate_grad = lax.optimization_barrier(jnp.sum(hidden_grad * gelu_val, axis=1))
    pre_grad = (hidden_grad * gelu_slope).astype(jnp.bfloat16)
    slot_grad = lax.dot_general(pre_grad, weight_in, (((1,), (1,)), ((), ())), preferred_element_type=jnp.float32)
    return (slot_grad.astype(jnp.bfloat16), gate_grad)

def block_ref(grad_in, feats, frame_mask, routed, slot_pos, preact, conv_k, gain_vec, cent_table, weight_in, weight_out, source):
    conv_f = conv_k.astype(jnp.float32)
    gain_f = gain_vec.astype(jnp.float32)
    feats3 = feats.astype(jnp.float32).reshape(UTTS, FRAMES_DEV, D)
    pre_act = time_conv(feats3 * frame_mask, conv_f, KER // 2)
    sig_pre = jax.nn.sigmoid(pre_act)
    residual = (feats3 + frame_mask * pre_act * sig_pre).reshape(FRAMES, D)
    inv_rms = lax.rsqrt(lax.optimization_barrier(jnp.mean(residual * residual, axis=1, keepdims=True)) + 1e-06)
    normed = (residual * inv_rms * gain_f).astype(jnp.bfloat16)
    score_all = jnp.dot(normed, cent_table.T, preferred_element_type=jnp.float32)
    score_val = jnp.take_along_axis(score_all, routed[:, None], axis=1)[:, 0]
    gate_val = jax.nn.sigmoid(score_val)
    cent_rows = cent_table[routed].astype(jnp.float32)
    position = (routed * SLOTS + source * CAP + slot_pos).astype(jnp.int32)
    bucket = jnp.zeros((EXPERTS * SLOTS, D), jnp.bfloat16).at[position].set(grad_in)
    grads_all, gates_all = lax.map(expert_back, (bucket.reshape(EXPERTS, SLOTS, D), preact.reshape(EXPERTS, SLOTS, HID), weight_in, weight_out))
    slot_grad = grads_all.reshape(EXPERTS * SLOTS, D)[position].astype(jnp.float32)
    gate_grad = gates_all.reshape(EXPERTS * SLOTS)[position]
    total_grad = gate_val[:, None] * slot_grad + (gate_val * (1.0 - gate_val) * gate_grad)[:, None] * cent_rows
    scaled = total_grad * gain_f
    cubed = inv_rms * inv_rms * inv_rms
    resid_grad = grad_in.astype(jnp.float32) + inv_rms * scaled - residual * cubed * lax.optimization_barrier(jnp.mean(residual * scaled, axis=1, keepdims=True))
    resid3 = resid_grad.reshape(UTTS, FRAMES_DEV, D)
    conv_slope = frame_mask * sig_pre * (1.0 + pre_act * (1.0 - sig_pre))
    conv_back = time_conv(conv_slope * resid3, conv_f[::-1], KER - 1 - KER // 2)
    return (resid3 + frame_mask * conv_back).reshape(FRAMES, D).astype(jnp.bfloat16)

def reference(feat_saved, out_grad, lengths, expert_ids, slot_ids, expert_preact, conv_weight, norm_gain, centroids, w_in, w_out):
    frame_pos = jnp.arange(FRAMES_DEV).astype(jnp.int32)
    source = (jnp.arange(FRAMES) // FRAMES_DEV).astype(jnp.int32)
    results = [[None] * MICRO for section_idx in range(SECTIONS)]
    for micro_idx in range(MICRO):
        frame_mask = (frame_pos[None, :] < lengths[micro_idx][:, None]).astype(jnp.float32)[:, :, None]
        grad_now = out_grad[micro_idx]
        for section_idx in reversed(range(SECTIONS)):
            grad_now = block_ref(grad_now, feat_saved[section_idx, micro_idx], frame_mask, expert_ids[section_idx, micro_idx], slot_ids[section_idx, micro_idx], expert_preact[section_idx, micro_idx], conv_weight[section_idx], norm_gain[section_idx], centroids[section_idx], w_in[section_idx], w_out[section_idx], source)
            results[section_idx][micro_idx] = grad_now
    return jnp.stack([jnp.stack(section_row) for section_row in results])
```

```python
import functools
import math

import jax
import jax.numpy as jnp
from jax import lax
from jax.experimental import pallas as pl
from jax.experimental.pallas import tpu as pltpu
from jax.sharding import PartitionSpec as P

LANES = 128
SUB = 8
MESH = pl.DeviceIdType.MESH


def contract_last(left, right):
    return lax.dot_general(
        left, right, (((1,), (1,)), ((), ())), preferred_element_type=jnp.float32
    )


def to_column(row):
    size = row.shape[1]
    same = lax.broadcasted_iota(jnp.int32, (size, size), 0) == lax.broadcasted_iota(
        jnp.int32, (size, size), 1
    )
    wide = jnp.broadcast_to(row.astype(jnp.float32), (size, size))
    return jnp.sum(jnp.where(same, wide, 0.0), axis=1, keepdims=True).astype(jnp.int32)


def kernel(
    axis,
    n,
    slot_cap,
    length_ref,
    routed_ref,
    slot_ref,
    conv_ref,
    gain_ref,
    cent_ref,
    feat_hbm,
    grad_hbm,
    preact_hbm,
    w_in_hbm,
    w_out_hbm,
    out_hbm,
    feat_ref,
    grad_ref,
    preact_ref,
    w_in_ref,
    w_out_ref,
    out_ref,
    taps_ref,
    gain_f,
    send_ref,
    recv_ref,
    back_ref,
    home_ref,
    gate_send,
    gate_recv,
    turn_ref,
    rows_ref,
    pad_ref,
    resid_ref,
    slope_ref,
    cent_rows,
    gelu_ref,
    gelu_slope_ref,
    slot_back,
    load_sem,
    out_sem,
    send_sem,
    recv_sem,
    back_sem,
    home_sem,
    gate_send_sem,
    gate_recv_sem,
):
    micro, frames, width = feat_ref.shape
    chunks = width // LANES
    slots = n * slot_cap
    tap_count = conv_ref.shape[0]
    low = tap_count // 2
    experts = n
    gate_span = LANES // micro
    me = lax.axis_index(axis)

    barrier = pltpu.get_barrier_semaphore()

    def greet(step, carry):
        pl.semaphore_signal(
            barrier, inc=1, device_id={axis: lax.rem(me + step, n)}, device_id_type=MESH
        )
        return carry

    def load(src, dst, at):
        return pltpu.make_async_copy(src, dst, load_sem.at[at])

    grad_loads = [load(grad_hbm.at[m], grad_ref.at[m], m) for m in range(micro)]
    feat_loads = [load(feat_hbm.at[m], feat_ref.at[m], micro + m) for m in range(micro)]
    pre_load = load(preact_hbm, preact_ref, 2 * micro)
    out_load = load(w_out_hbm, w_out_ref, 2 * micro + 1)
    in_load = load(w_in_hbm, w_in_ref, 2 * micro + 2)
    for copy in (*grad_loads, *feat_loads, pre_load, out_load, in_load):
        copy.start()
    lax.fori_loop(1, n, greet, 0)

    def cols(c):
        return pl.ds(c * LANES, LANES)

    def to_blocks(rows, dst):
        for c in range(chunks):
            turn_ref[pl.ds(c, slots, stride=chunks), :] = rows[:, c * LANES : (c + 1) * LANES]
        dst[...] = turn_ref[...].astype(jnp.bfloat16).reshape(dst.shape)

    def from_blocks(src):
        turn_ref[...] = src[...].reshape(turn_ref.shape).astype(jnp.float32)
        for c in range(chunks):
            rows_ref[:, cols(c)] = turn_ref[pl.ds(c, slots, stride=chunks), :].astype(jnp.bfloat16)

    def exchange(src, dst, sent, got):
        def post(step, carry):
            peer = lax.rem(me + step, n)
            pltpu.make_async_remote_copy(
                src_ref=src.at[peer],
                dst_ref=dst.at[me],
                send_sem=sent,
                recv_sem=got,
                device_id={axis: peer},
                device_id_type=MESH,
            ).start()
            return carry

        lax.fori_loop(1, n, post, 0)
        pltpu.make_async_copy(src.at[me], dst.at[me], got).start()

    def arrived(dst, got):
        pltpu.make_async_copy(dst, dst, got).wait()

    def departed(src, sent):
        part = src.at[pl.ds(0, n - 1)]
        pltpu.make_async_copy(part, part, sent).wait()

    for m in range(micro):
        grad_loads[m].wait()
        target = routed_ref[m : m + 1, :] * slot_cap + slot_ref[m : m + 1, :]
        onehot = (lax.broadcasted_iota(jnp.int32, (slots, frames), 0) == target).astype(
            jnp.float32
        ).astype(jnp.bfloat16)
        bucket = jnp.dot(onehot, grad_ref[m], preferred_element_type=jnp.float32)
        to_blocks(bucket, send_ref.at[m])
        if m == 0:
            pl.semaphore_wait(barrier, n - 1)
        exchange(send_ref.at[m], recv_ref.at[m], send_sem.at[m], recv_sem.at[m])

    for c in range(chunks):
        taps_ref[c] = conv_ref[:, cols(c)].astype(jnp.float32)
        gain_f[c] = gain_ref[:, cols(c)].astype(jnp.float32)
        pad_ref[c, 0:low, :] = jnp.zeros((low, LANES), jnp.float32)
        pad_ref[c, low + frames :, :] = jnp.zeros((tap_count - low, LANES), jnp.float32)

    frame_at = lax.broadcasted_iota(jnp.int32, (frames, 1), 0)

    masks, inv_all, gate_all, exp_all, slot_all, slot_hot = [], [], [], [], [], []
    for m in range(micro):
        feat_loads[m].wait()
        mask = (frame_at < length_ref[m, 0]).astype(jnp.float32)
        routed = to_column(routed_ref[m : m + 1, :])
        slot_pos = to_column(slot_ref[m : m + 1, :])
        exp_hot = (
            lax.broadcasted_iota(jnp.int32, (frames, experts), 1) == routed
        ).astype(jnp.float32)
        cent_rows[m] = jnp.dot(
            exp_hot.astype(jnp.bfloat16), cent_ref[...], preferred_element_type=jnp.float32
        ).astype(jnp.bfloat16)

        def ahead(c, square):
            lanes = pl.ds(pl.multiple_of(c * LANES, LANES), LANES)
            feats = feat_ref[m, :, lanes].astype(jnp.float32)
            pad_ref[c, low : low + frames, :] = feats * mask
            acc = jnp.zeros((frames, LANES), jnp.float32)
            for k in range(tap_count):
                acc = acc + taps_ref[c, k : k + 1, :] * pad_ref[c, k : k + frames, :]
            sig = jax.nn.sigmoid(acc)
            resid = feats + mask * acc * sig
            resid_ref[m, c] = resid
            slope_ref[m, c] = mask * sig * (1.0 + acc * (1.0 - sig))
            return square + resid * resid

        square = lax.fori_loop(0, chunks, ahead, jnp.zeros((frames, LANES), jnp.float32))
        inv_rms = lax.rsqrt(jnp.sum(square, axis=1, keepdims=True) * (1.0 / width) + 1e-06)

        def scoring(c, total):
            lanes = pl.ds(pl.multiple_of(c * LANES, LANES), LANES)
            normed = (resid_ref[m, c] * inv_rms * gain_f[c]).astype(jnp.bfloat16)
            return total + normed.astype(jnp.float32) * cent_rows[m, :, lanes].astype(jnp.float32)

        score = lax.fori_loop(0, chunks, scoring, jnp.zeros((frames, LANES), jnp.float32))
        gate_all.append(jax.nn.sigmoid(jnp.sum(score, axis=1, keepdims=True)))
        masks.append(mask)
        inv_all.append(inv_rms)
        exp_all.append(exp_hot)
        slot_all.append(slot_pos)
        slot_hot.append(
            (
                lax.broadcasted_iota(jnp.int32, (frames, slots), 1)
                == routed * slot_cap + slot_pos
            ).astype(jnp.float32).astype(jnp.bfloat16)
        )

        if m == 0:
            pre_load.wait()
        act = preact_ref[m].astype(jnp.float32)
        cdf = 0.5 * (1.0 + lax.erf(act * (1.0 / math.sqrt(2.0))))
        gelu_ref[m] = act * cdf
        gelu_slope_ref[m] = cdf + act * jnp.exp(-0.5 * act * act) * (
            1.0 / math.sqrt(2.0 * math.pi)
        )

    out_load.wait()
    in_load.wait()
    gate_rows = jnp.zeros((n, LANES), jnp.float32)
    slot_id = lax.broadcasted_iota(jnp.int32, (slots, LANES), 0)
    lane_id = lax.broadcasted_iota(jnp.int32, (slots, LANES), 1)
    group_first = lax.broadcasted_iota(jnp.int32, (n, slots), 0) * slot_cap
    group_slot = lax.broadcasted_iota(jnp.int32, (n, slots), 1)
    grouped = jnp.logical_and(
        group_slot >= group_first, group_slot < group_first + slot_cap
    ).astype(jnp.float32)
    for m in range(micro):
        arrived(recv_ref.at[m], recv_sem.at[m])
        from_blocks(recv_ref.at[m])
        hidden = contract_last(rows_ref[...], w_out_ref[...])
        gate = jnp.sum(hidden * gelu_ref[m], axis=1, keepdims=True)
        pre_grad = (hidden * gelu_slope_ref[m]).astype(jnp.bfloat16)
        to_blocks(contract_last(pre_grad, w_in_ref[...]), back_ref.at[m])
        exchange(back_ref.at[m], home_ref.at[m], back_sem.at[m], home_sem.at[m])
        spread = jnp.where(lax.rem(slot_id, slot_cap) + m * gate_span == lane_id, gate, 0.0)
        gate_rows = gate_rows + jnp.dot(
            grouped, spread, preferred_element_type=jnp.float32, precision=lax.Precision.HIGHEST
        )
    gate_send[...] = gate_rows.reshape(gate_send.shape)
    exchange(gate_send, gate_recv, gate_send_sem, gate_recv_sem)
    arrived(gate_recv, gate_recv_sem)
    gate_home = gate_recv[...].reshape(n, LANES)

    frame_lane = lax.broadcasted_iota(jnp.int32, (frames, LANES), 1)
    for m in range(micro):
        mask, inv_rms, gate_val = masks[m], inv_all[m], gate_all[m]
        picked = jnp.dot(
            exp_all[m],
            gate_home,
            preferred_element_type=jnp.float32,
            precision=lax.Precision.HIGHEST,
        )
        gate_grad = jnp.sum(
            jnp.where(frame_lane == slot_all[m] + m * gate_span, picked, 0.0),
            axis=1,
            keepdims=True,
        )
        cent_scale = gate_val * (1.0 - gate_val) * gate_grad
        arrived(home_ref.at[m], home_sem.at[m])
        from_blocks(home_ref.at[m])
        slot_back[...] = jnp.dot(slot_hot[m], rows_ref[...], preferred_element_type=jnp.float32)

        def scaling(c, total):
            lanes = pl.ds(pl.multiple_of(c * LANES, LANES), LANES)
            grad = gate_val * slot_back[:, lanes] + cent_scale * cent_rows[m, :, lanes].astype(
                jnp.float32
            )
            scaled = grad * gain_f[c]
            slot_back[:, lanes] = scaled
            return total + resid_ref[m, c] * scaled

        total = lax.fori_loop(0, chunks, scaling, jnp.zeros((frames, LANES), jnp.float32))
        mean = jnp.sum(total, axis=1, keepdims=True) * (1.0 / width)
        back_scale = inv_rms * inv_rms * inv_rms * mean

        def finish(c, carry):
            lanes = pl.ds(pl.multiple_of(c * LANES, LANES), LANES)
            resid_grad = (
                grad_ref[m, :, lanes].astype(jnp.float32)
                + inv_rms * slot_back[:, lanes]
                - resid_ref[m, c] * back_scale
            )
            pad_ref[c, low : low + frames, :] = slope_ref[m, c] * resid_grad
            acc = jnp.zeros((frames, LANES), jnp.float32)
            for k in range(tap_count):
                first = 2 * low - k
                acc = acc + taps_ref[c, k : k + 1, :] * pad_ref[c, first : first + frames, :]
            out_ref[m, :, lanes] = (resid_grad + mask * acc).astype(jnp.bfloat16)
            return carry

        lax.fori_loop(0, chunks, finish, 0)
        pltpu.make_async_copy(out_ref.at[m], out_hbm.at[m], out_sem.at[m]).start()

    for m in range(micro):
        departed(send_ref.at[m], send_sem.at[m])
        departed(back_ref.at[m], back_sem.at[m])
    departed(gate_send, gate_send_sem)
    for m in range(micro):
        pltpu.make_async_copy(out_ref.at[m], out_hbm.at[m], out_sem.at[m]).wait()


def block_grads(
    grads, feats, lengths, routed, slot_pos, preact, conv_k, gain, cent, weight_in, weight_out
):
    micro, frames, width = feats.shape
    n = lax.axis_size("expert")
    hidden = weight_in.shape[1]
    cap = preact.shape[1] // n
    whole_rows = 16 * LANES // math.gcd(16 * LANES, width)
    slot_cap = -(-cap // whole_rows) * whole_rows
    if slot_cap != cap:
        preact = jnp.pad(
            preact.reshape(micro, n, cap, hidden), ((0, 0), (0, 0), (0, slot_cap - cap), (0, 0))
        ).reshape(micro, n * slot_cap, hidden)
    slots = n * slot_cap
    chunks = width // LANES
    taps = conv_k.shape[0]
    block = (n, slot_cap * chunks, LANES)
    bf16, f32 = jnp.bfloat16, jnp.float32
    vmem = pl.BlockSpec(memory_space=pltpu.VMEM)
    smem = pl.BlockSpec(memory_space=pltpu.SMEM)
    anywhere = pl.BlockSpec(memory_space=pl.ANY)
    dma = pltpu.SemaphoreType.DMA
    flops = micro * (4 * slots * width * hidden + 4 * frames * width * (taps + slots))
    return pl.pallas_call(
        functools.partial(kernel, "expert", n, slot_cap),
        out_shape=jax.ShapeDtypeStruct((micro, frames, width), bf16),
        in_specs=[smem] + [vmem] * 5 + [anywhere] * 5,
        out_specs=anywhere,
        scratch_shapes=[
            pltpu.VMEM((micro, frames, width), bf16),
            pltpu.VMEM((micro, frames, width), bf16),
            pltpu.VMEM((micro, slots, hidden), bf16),
            pltpu.VMEM((width, hidden), bf16),
            pltpu.VMEM((hidden, width), bf16),
            pltpu.VMEM((micro, frames, width), bf16),
            pltpu.VMEM((chunks, taps, LANES), f32),
            pltpu.VMEM((chunks, 1, LANES), f32),
            pltpu.VMEM((micro, *block), bf16),
            pltpu.VMEM((micro, *block), bf16),
            pltpu.VMEM((micro, *block), bf16),
            pltpu.VMEM((micro, *block), bf16),
            pltpu.VMEM((n, 1, LANES), f32),
            pltpu.VMEM((n, 1, LANES), f32),
            pltpu.VMEM((slots * chunks, LANES), f32),
            pltpu.VMEM((slots, width), bf16),
            pltpu.VMEM((chunks, frames + taps, LANES), f32),
            pltpu.VMEM((micro, chunks, frames, LANES), f32),
            pltpu.VMEM((micro, chunks, frames, LANES), f32),
            pltpu.VMEM((micro, frames, width), bf16),
            pltpu.VMEM((micro, slots, hidden), f32),
            pltpu.VMEM((micro, slots, hidden), f32),
            pltpu.VMEM((frames, width), f32),
            dma((2 * micro + 3,)),
            dma((micro,)),
            dma((micro,)),
            dma((micro,)),
            dma((micro,)),
            dma((micro,)),
            dma,
            dma,
        ],
        compiler_params=pltpu.CompilerParams(
            collective_id=0, has_side_effects=True, vmem_limit_bytes=40 * 1024 * 1024
        ),
        cost_estimate=pl.CostEstimate(
            flops=flops, bytes_accessed=8 * 1024 * 1024, transcendentals=0
        ),
    )(lengths, routed, slot_pos, conv_k, gain, cent, feats, grads, preact, weight_in, weight_out)


def on_device(
    feat_saved,
    out_grad,
    lengths,
    expert_ids,
    slot_ids,
    expert_preact,
    conv_weight,
    norm_gain,
    centroids,
    w_in,
    w_out,
):
    section_count = lax.axis_size("section")
    micro_count = out_grad.shape[0]
    feats, routed, slots, preact = feat_saved[0], expert_ids[0], slot_ids[0], expert_preact[0]
    fixed = (conv_weight[0], norm_gain, centroids[0], w_in[0, 0], w_out[0, 0])
    if section_count == 1:
        return block_grads(out_grad, feats, lengths, routed, slots, preact, *fixed)[None]

    section_idx = lax.axis_index("section")
    route = [(i + 1, i) for i in range(section_count - 1)]

    def one_tick(tick_idx, carry):
        incoming, grads = carry
        micro_pos = tick_idx - (section_count - 1 - section_idx)
        is_valid = jnp.logical_and(micro_pos >= 0, micro_pos < micro_count)
        micro_sel = jnp.clip(micro_pos, 0, micro_count - 1)

        def pick(array):
            return lax.dynamic_slice_in_dim(array, micro_sel, 1, 0)

        grad_in = jnp.where(section_idx == section_count - 1, pick(out_grad), incoming)
        new_grad = block_grads(
            grad_in, pick(feats), pick(lengths), pick(routed), pick(slots), pick(preact), *fixed
        )
        updated = lax.dynamic_update_slice_in_dim(grads, new_grad, micro_sel, 0)
        grads = jnp.where(is_valid, updated, grads)
        return (lax.ppermute(new_grad, "section", route), grads)

    start = (jnp.zeros((1, *out_grad.shape[1:]), jnp.bfloat16), jnp.zeros_like(out_grad))
    _, grads = lax.fori_loop(0, section_count + micro_count - 1, one_tick, start)
    return grads[None]


def solution(mesh):
    in_specs = (
        P("section", None, "expert", None),
        P(None, "expert", None),
        P(None, "expert"),
        P("section", None, "expert"),
        P("section", None, "expert"),
        P("section", None, "expert", None),
        P("section", None, None),
        P("section", None),
        P("section", None, None),
        P("section", "expert", None, None),
        P("section", "expert", None, None),
    )
    out_specs = P("section", None, "expert", None)
    return jax.shard_map(
        on_device, mesh=mesh, in_specs=in_specs, out_specs=out_specs, check_vma=False
    )
```

```python
import functools
import math

import jax
import jax.numpy as jnp
from jax import lax
from jax.experimental import pallas as pl
from jax.experimental.pallas import tpu as pltpu
from jax.sharding import PartitionSpec as P

LANES = 128
SUB = 8
MESH = pl.DeviceIdType.MESH


def contract_last(left, right):
    return lax.dot_general(
        left, right, (((1,), (1,)), ((), ())), preferred_element_type=jnp.float32
    )


def to_column(row):
    size = row.shape[1]
    same = lax.broadcasted_iota(jnp.int32, (size, size), 0) == lax.broadcasted_iota(
        jnp.int32, (size, size), 1
    )
    wide = jnp.broadcast_to(row.astype(jnp.float32), (size, size))
    return jnp.sum(jnp.where(same, wide, 0.0), axis=1, keepdims=True).astype(jnp.int32)


def kernel(
    axis,
    n,
    slot_cap,
    length_hbm,
    routed_hbm,
    slot_hbm,
    conv_hbm,
    gain_hbm,
    cent_hbm,
    feat_hbm,
    grad_hbm,
    preact_hbm,
    w_in_hbm,
    w_out_hbm,
    out_hbm,
    length_ref,
    routed_ref,
    slot_ref,
    conv_ref,
    gain_ref,
    cent_ref,
    feat_ref,
    grad_ref,
    preact_ref,
    w_in_ref,
    w_out_ref,
    out_ref,
    taps_ref,
    gain_f,
    send_ref,
    recv_ref,
    back_ref,
    home_ref,
    gate_send,
    gate_recv,
    turn_ref,
    rows_ref,
    pad_ref,
    resid_ref,
    slope_ref,
    cent_rows,
    gelu_ref,
    gelu_slope_ref,
    slot_back,
    load_sem,
    out_sem,
    send_sem,
    recv_sem,
    back_sem,
    home_sem,
    gate_send_sem,
    gate_recv_sem,
):
    micro, frames, width = feat_ref.shape
    chunks = width // LANES
    slots = n * slot_cap
    tap_count = conv_ref.shape[0]
    low = tap_count // 2
    experts = n
    gate_span = LANES // micro
    me = lax.axis_index(axis)

    barrier = pltpu.get_barrier_semaphore()

    def greet(step, carry):
        pl.semaphore_signal(
            barrier, inc=1, device_id={axis: lax.rem(me + step, n)}, device_id_type=MESH
        )
        return carry

    def load(src, dst, at):
        return pltpu.make_async_copy(src, dst, load_sem.at[at])

    routed_load = load(routed_hbm, routed_ref, 2 * micro + 3)
    slot_load = load(slot_hbm, slot_ref, 2 * micro + 4)
    small_loads = [
        load(conv_hbm, conv_ref, 2 * micro + 5),
        load(gain_hbm, gain_ref, 2 * micro + 6),
        load(cent_hbm, cent_ref, 2 * micro + 7),
        load(length_hbm, length_ref, 2 * micro + 8),
    ]
    grad_loads = [load(grad_hbm.at[m], grad_ref.at[m], m) for m in range(micro)]
    feat_loads = [load(feat_hbm.at[m], feat_ref.at[m], micro + m) for m in range(micro)]
    pre_load = load(preact_hbm, preact_ref, 2 * micro)
    out_load = load(w_out_hbm, w_out_ref, 2 * micro + 1)
    in_load = load(w_in_hbm, w_in_ref, 2 * micro + 2)
    for copy in (routed_load, slot_load, *grad_loads):
        copy.start()
    lax.fori_loop(1, n, greet, 0)
    for copy in (*small_loads, *feat_loads, pre_load, out_load, in_load):
        copy.start()

    def cols(c):
        return pl.ds(c * LANES, LANES)

    def to_blocks(rows, dst):
        for c in range(chunks):
            turn_ref[pl.ds(c, slots, stride=chunks), :] = rows[:, c * LANES : (c + 1) * LANES]
        dst[...] = turn_ref[...].astype(jnp.bfloat16).reshape(dst.shape)

    def from_blocks(src):
        turn_ref[...] = src[...].reshape(turn_ref.shape).astype(jnp.float32)
        for c in range(chunks):
            rows_ref[:, cols(c)] = turn_ref[pl.ds(c, slots, stride=chunks), :].astype(jnp.bfloat16)

    def exchange(src, dst, sent, got):
        def post(step, carry):
            peer = lax.rem(me + step, n)
            pltpu.make_async_remote_copy(
                src_ref=src.at[peer],
                dst_ref=dst.at[me],
                send_sem=sent,
                recv_sem=got,
                device_id={axis: peer},
                device_id_type=MESH,
            ).start()
            return carry

        lax.fori_loop(1, n, post, 0)
        pltpu.make_async_copy(src.at[me], dst.at[me], got).start()

    def arrived(dst, got):
        pltpu.make_async_copy(dst, dst, got).wait()

    def departed(src, sent):
        part = src.at[pl.ds(0, n - 1)]
        pltpu.make_async_copy(part, part, sent).wait()

    routed_load.wait()
    slot_load.wait()
    for m in range(micro):
        grad_loads[m].wait()
        target = routed_ref[m : m + 1, :] * slot_cap + slot_ref[m : m + 1, :]
        onehot = (lax.broadcasted_iota(jnp.int32, (slots, frames), 0) == target).astype(
            jnp.float32
        ).astype(jnp.bfloat16)
        bucket = jnp.dot(onehot, grad_ref[m], preferred_element_type=jnp.float32)
        to_blocks(bucket, send_ref.at[m])
        if m == 0:
            pl.semaphore_wait(barrier, n - 1)
        exchange(send_ref.at[m], recv_ref.at[m], send_sem.at[m], recv_sem.at[m])

    for copy in small_loads:
        copy.wait()

    for c in range(chunks):
        taps_ref[c] = conv_ref[:, cols(c)].astype(jnp.float32)
        gain_f[c] = gain_ref[:, cols(c)].astype(jnp.float32)
        pad_ref[c, 0:low, :] = jnp.zeros((low, LANES), jnp.float32)
        pad_ref[c, low + frames :, :] = jnp.zeros((tap_count - low, LANES), jnp.float32)

    frame_at = lax.broadcasted_iota(jnp.int32, (frames, 1), 0)

    masks, inv_all, gate_all, exp_all, slot_all, slot_hot = [], [], [], [], [], []
    for m in range(micro):
        feat_loads[m].wait()
        mask = (frame_at < length_ref[0, m]).astype(jnp.float32)
        routed = to_column(routed_ref[m : m + 1, :])
        slot_pos = to_column(slot_ref[m : m + 1, :])
        exp_hot = (
            lax.broadcasted_iota(jnp.int32, (frames, experts), 1) == routed
        ).astype(jnp.float32)
        cent_rows[m] = jnp.dot(
            exp_hot.astype(jnp.bfloat16), cent_ref[...], preferred_element_type=jnp.float32
        ).astype(jnp.bfloat16)

        def ahead(c, square):
            lanes = pl.ds(pl.multiple_of(c * LANES, LANES), LANES)
            feats = feat_ref[m, :, lanes].astype(jnp.float32)
            pad_ref[c, low : low + frames, :] = feats * mask
            acc = jnp.zeros((frames, LANES), jnp.float32)
            for k in range(tap_count):
                acc = acc + taps_ref[c, k : k + 1, :] * pad_ref[c, k : k + frames, :]
            sig = jax.nn.sigmoid(acc)
            resid = feats + mask * acc * sig
            resid_ref[m, c] = resid
            slope_ref[m, c] = mask * sig * (1.0 + acc * (1.0 - sig))
            return square + resid * resid

        square = lax.fori_loop(0, chunks, ahead, jnp.zeros((frames, LANES), jnp.float32))
        inv_rms = lax.rsqrt(jnp.sum(square, axis=1, keepdims=True) * (1.0 / width) + 1e-06)

        def scoring(c, total):
            lanes = pl.ds(pl.multiple_of(c * LANES, LANES), LANES)
            normed = (resid_ref[m, c] * inv_rms * gain_f[c]).astype(jnp.bfloat16)
            return total + normed.astype(jnp.float32) * cent_rows[m, :, lanes].astype(jnp.float32)

        score = lax.fori_loop(0, chunks, scoring, jnp.zeros((frames, LANES), jnp.float32))
        gate_all.append(jax.nn.sigmoid(jnp.sum(score, axis=1, keepdims=True)))
        masks.append(mask)
        inv_all.append(inv_rms)
        exp_all.append(exp_hot)
        slot_all.append(slot_pos)
        slot_hot.append(
            (
                lax.broadcasted_iota(jnp.int32, (frames, slots), 1)
                == routed * slot_cap + slot_pos
            ).astype(jnp.float32).astype(jnp.bfloat16)
        )

        if m == 0:
            pre_load.wait()
        act = preact_ref[m].astype(jnp.float32)
        cdf = 0.5 * (1.0 + lax.erf(act * (1.0 / math.sqrt(2.0))))
        gelu_ref[m] = act * cdf
        gelu_slope_ref[m] = cdf + act * jnp.exp(-0.5 * act * act) * (
            1.0 / math.sqrt(2.0 * math.pi)
        )

    out_load.wait()
    in_load.wait()
    gate_rows = jnp.zeros((n, LANES), jnp.float32)
    slot_id = lax.broadcasted_iota(jnp.int32, (slots, LANES), 0)
    lane_id = lax.broadcasted_iota(jnp.int32, (slots, LANES), 1)
    group_first = lax.broadcasted_iota(jnp.int32, (n, slots), 0) * slot_cap
    group_slot = lax.broadcasted_iota(jnp.int32, (n, slots), 1)
    grouped = jnp.logical_and(
        group_slot >= group_first, group_slot < group_first + slot_cap
    ).astype(jnp.float32)
    for m in range(micro):
        arrived(recv_ref.at[m], recv_sem.at[m])
        from_blocks(recv_ref.at[m])
        hidden = contract_last(rows_ref[...], w_out_ref[...])
        gate = jnp.sum(hidden * gelu_ref[m], axis=1, keepdims=True)
        pre_grad = (hidden * gelu_slope_ref[m]).astype(jnp.bfloat16)
        to_blocks(contract_last(pre_grad, w_in_ref[...]), back_ref.at[m])
        exchange(back_ref.at[m], home_ref.at[m], back_sem.at[m], home_sem.at[m])
        spread = jnp.where(lax.rem(slot_id, slot_cap) + m * gate_span == lane_id, gate, 0.0)
        gate_rows = gate_rows + jnp.dot(
            grouped, spread, preferred_element_type=jnp.float32, precision=lax.Precision.HIGHEST
        )
    gate_send[...] = gate_rows.reshape(gate_send.shape)
    exchange(gate_send, gate_recv, gate_send_sem, gate_recv_sem)
    arrived(gate_recv, gate_recv_sem)
    gate_home = gate_recv[...].reshape(n, LANES)

    frame_lane = lax.broadcasted_iota(jnp.int32, (frames, LANES), 1)
    for m in range(micro):
        mask, inv_rms, gate_val = masks[m], inv_all[m], gate_all[m]
        picked = jnp.dot(
            exp_all[m],
            gate_home,
            preferred_element_type=jnp.float32,
            precision=lax.Precision.HIGHEST,
        )
        gate_grad = jnp.sum(
            jnp.where(frame_lane == slot_all[m] + m * gate_span, picked, 0.0),
            axis=1,
            keepdims=True,
        )
        cent_scale = gate_val * (1.0 - gate_val) * gate_grad
        arrived(home_ref.at[m], home_sem.at[m])
        from_blocks(home_ref.at[m])
        slot_back[...] = jnp.dot(slot_hot[m], rows_ref[...], preferred_element_type=jnp.float32)

        def scaling(c, total):
            lanes = pl.ds(pl.multiple_of(c * LANES, LANES), LANES)
            grad = gate_val * slot_back[:, lanes] + cent_scale * cent_rows[m, :, lanes].astype(
                jnp.float32
            )
            scaled = grad * gain_f[c]
            slot_back[:, lanes] = scaled
            return total + resid_ref[m, c] * scaled

        total = lax.fori_loop(0, chunks, scaling, jnp.zeros((frames, LANES), jnp.float32))
        mean = jnp.sum(total, axis=1, keepdims=True) * (1.0 / width)
        back_scale = inv_rms * inv_rms * inv_rms * mean

        def finish(c, carry):
            lanes = pl.ds(pl.multiple_of(c * LANES, LANES), LANES)
            resid_grad = (
                grad_ref[m, :, lanes].astype(jnp.float32)
                + inv_rms * slot_back[:, lanes]
                - resid_ref[m, c] * back_scale
            )
            pad_ref[c, low : low + frames, :] = slope_ref[m, c] * resid_grad
            acc = jnp.zeros((frames, LANES), jnp.float32)
            for k in range(tap_count):
                first = 2 * low - k
                acc = acc + taps_ref[c, k : k + 1, :] * pad_ref[c, first : first + frames, :]
            out_ref[m, :, lanes] = (resid_grad + mask * acc).astype(jnp.bfloat16)
            return carry

        lax.fori_loop(0, chunks, finish, 0)
        pltpu.make_async_copy(out_ref.at[m], out_hbm.at[m], out_sem.at[m]).start()

    for m in range(micro):
        departed(send_ref.at[m], send_sem.at[m])
        departed(back_ref.at[m], back_sem.at[m])
    departed(gate_send, gate_send_sem)
    for m in range(micro):
        pltpu.make_async_copy(out_ref.at[m], out_hbm.at[m], out_sem.at[m]).wait()


def block_grads(
    grads, feats, lengths, routed, slot_pos, preact, conv_k, gain, cent, weight_in, weight_out
):
    micro, frames, width = feats.shape
    n = lax.axis_size("expert")
    hidden = weight_in.shape[1]
    cap = preact.shape[1] // n
    whole_rows = 16 * LANES // math.gcd(16 * LANES, width)
    slot_cap = -(-cap // whole_rows) * whole_rows
    if slot_cap != cap:
        preact = jnp.pad(
            preact.reshape(micro, n, cap, hidden), ((0, 0), (0, 0), (0, slot_cap - cap), (0, 0))
        ).reshape(micro, n * slot_cap, hidden)
    slots = n * slot_cap
    chunks = width // LANES
    taps = conv_k.shape[0]
    block = (n, slot_cap * chunks, LANES)
    bf16, f32 = jnp.bfloat16, jnp.float32
    in_hbm = pl.BlockSpec(memory_space=pltpu.HBM)
    anywhere = pl.BlockSpec(memory_space=pl.ANY)
    dma = pltpu.SemaphoreType.DMA
    flops = micro * (4 * slots * width * hidden + 4 * frames * width * (taps + slots))
    return pl.pallas_call(
        functools.partial(kernel, "expert", n, slot_cap),
        out_shape=jax.ShapeDtypeStruct((micro, frames, width), bf16),
        in_specs=[in_hbm] * 11,
        out_specs=anywhere,
        scratch_shapes=[
            pltpu.SMEM((1, micro), jnp.int32),
            pltpu.VMEM((micro, frames), jnp.int32),
            pltpu.VMEM((micro, frames), jnp.int32),
            pltpu.VMEM((taps, width), bf16),
            pltpu.VMEM((1, width), bf16),
            pltpu.VMEM((n, width), bf16),
            pltpu.VMEM((micro, frames, width), bf16),
            pltpu.VMEM((micro, frames, width), bf16),
            pltpu.VMEM((micro, slots, hidden), bf16),
            pltpu.VMEM((width, hidden), bf16),
            pltpu.VMEM((hidden, width), bf16),
            pltpu.VMEM((micro, frames, width), bf16),
            pltpu.VMEM((chunks, taps, LANES), f32),
            pltpu.VMEM((chunks, 1, LANES), f32),
            pltpu.VMEM((micro, *block), bf16),
            pltpu.VMEM((micro, *block), bf16),
            pltpu.VMEM((micro, *block), bf16),
            pltpu.VMEM((micro, *block), bf16),
            pltpu.VMEM((n, 1, LANES), f32),
            pltpu.VMEM((n, 1, LANES), f32),
            pltpu.VMEM((slots * chunks, LANES), f32),
            pltpu.VMEM((slots, width), bf16),
            pltpu.VMEM((chunks, frames + taps, LANES), f32),
            pltpu.VMEM((micro, chunks, frames, LANES), f32),
            pltpu.VMEM((micro, chunks, frames, LANES), f32),
            pltpu.VMEM((micro, frames, width), bf16),
            pltpu.VMEM((micro, slots, hidden), f32),
            pltpu.VMEM((micro, slots, hidden), f32),
            pltpu.VMEM((frames, width), f32),
            dma((2 * micro + 9,)),
            dma((micro,)),
            dma((micro,)),
            dma((micro,)),
            dma((micro,)),
            dma((micro,)),
            dma,
            dma,
        ],
        compiler_params=pltpu.CompilerParams(
            collective_id=0, has_side_effects=True, vmem_limit_bytes=60 * 1024 * 1024
        ),
        cost_estimate=pl.CostEstimate(
            flops=flops, bytes_accessed=8 * 1024 * 1024, transcendentals=0
        ),
    )(lengths.reshape(1, micro), routed, slot_pos, conv_k, gain, cent, feats, grads, preact, weight_in, weight_out)


def on_device(
    feat_saved,
    out_grad,
    lengths,
    expert_ids,
    slot_ids,
    expert_preact,
    conv_weight,
    norm_gain,
    centroids,
    w_in,
    w_out,
):
    section_count = lax.axis_size("section")
    micro_count = out_grad.shape[0]
    feats, routed, slots, preact = feat_saved[0], expert_ids[0], slot_ids[0], expert_preact[0]
    fixed = (conv_weight[0], norm_gain, centroids[0], w_in[0, 0], w_out[0, 0])
    if section_count == 1:
        return block_grads(out_grad, feats, lengths, routed, slots, preact, *fixed)[None]

    section_idx = lax.axis_index("section")
    route = [(i + 1, i) for i in range(section_count - 1)]

    def one_tick(tick_idx, carry):
        incoming, grads = carry
        micro_pos = tick_idx - (section_count - 1 - section_idx)
        is_valid = jnp.logical_and(micro_pos >= 0, micro_pos < micro_count)
        micro_sel = jnp.clip(micro_pos, 0, micro_count - 1)

        def pick(array):
            return lax.dynamic_slice_in_dim(array, micro_sel, 1, 0)

        grad_in = jnp.where(section_idx == section_count - 1, pick(out_grad), incoming)
        new_grad = block_grads(
            grad_in, pick(feats), pick(lengths), pick(routed), pick(slots), pick(preact), *fixed
        )
        updated = lax.dynamic_update_slice_in_dim(grads, new_grad, micro_sel, 0)
        grads = jnp.where(is_valid, updated, grads)
        return (lax.ppermute(new_grad, "section", route), grads)

    start = (jnp.zeros((1, *out_grad.shape[1:]), jnp.bfloat16), jnp.zeros_like(out_grad))
    _, grads = lax.fori_loop(0, section_count + micro_count - 1, one_tick, start)
    return grads[None]


def solution(mesh):
    in_specs = (
        P("section", None, "expert", None),
        P(None, "expert", None),
        P(None, "expert"),
        P("section", None, "expert"),
        P("section", None, "expert"),
        P("section", None, "expert", None),
        P("section", None, None),
        P("section", None),
        P("section", None, None),
        P("section", "expert", None, None),
        P("section", "expert", None, None),
    )
    out_specs = P("section", None, "expert", None)
    return jax.shard_map(
        on_device, mesh=mesh, in_specs=in_specs, out_specs=out_specs, check_vma=False
    )
```

```python
import functools
import math

import jax
import jax.numpy as jnp
from jax import lax
from jax.experimental import pallas as pl
from jax.experimental.pallas import tpu as pltpu
from jax.sharding import PartitionSpec as P

LANES = 128
SUB = 8
MESH = pl.DeviceIdType.MESH


def contract_last(left, right):
    return lax.dot_general(
        left, right, (((1,), (1,)), ((), ())), preferred_element_type=jnp.float32
    )


def to_column(row):
    size = row.shape[1]
    same = lax.broadcasted_iota(jnp.int32, (size, size), 0) == lax.broadcasted_iota(
        jnp.int32, (size, size), 1
    )
    wide = jnp.broadcast_to(row.astype(jnp.float32), (size, size))
    return jnp.sum(jnp.where(same, wide, 0.0), axis=1, keepdims=True).astype(jnp.int32)


def kernel(
    axis,
    n,
    slot_cap,
    length_hbm,
    routed_hbm,
    slot_hbm,
    conv_hbm,
    gain_hbm,
    cent_hbm,
    feat_hbm,
    grad_hbm,
    preact_hbm,
    w_in_hbm,
    w_out_hbm,
    out_hbm,
    length_ref,
    routed_ref,
    slot_ref,
    conv_ref,
    gain_ref,
    cent_ref,
    feat_ref,
    grad_ref,
    preact_ref,
    w_in_ref,
    w_out_ref,
    out_ref,
    taps_ref,
    gain_f,
    send_ref,
    recv_ref,
    back_ref,
    home_ref,
    gate_send,
    gate_recv,
    turn_ref,
    rows_ref,
    pad_ref,
    resid_ref,
    slope_ref,
    cent_rows,
    gelu_ref,
    gelu_slope_ref,
    slot_back,
    load_sem,
    out_sem,
    send_sem,
    recv_sem,
    back_sem,
    home_sem,
    gate_send_sem,
    gate_recv_sem,
):
    micro, frames, width = feat_ref.shape
    stride = next(k for k in range(n // 3 + 1, 2 * n) if math.gcd(k, n) == 1)
    chunks = width // LANES
    slots = n * slot_cap
    tap_count = conv_ref.shape[0]
    low = tap_count // 2
    experts = n
    me = lax.axis_index(axis)

    barrier = pltpu.get_barrier_semaphore()

    def greet(step, carry):
        pl.semaphore_signal(
            barrier, inc=1, device_id={axis: lax.rem(me + step, n)}, device_id_type=MESH
        )
        return carry

    def load(src, dst, at):
        return pltpu.make_async_copy(src, dst, load_sem.at[at])

    routed_load = load(routed_hbm, routed_ref, 2 * micro + 3)
    slot_load = load(slot_hbm, slot_ref, 2 * micro + 4)
    small_loads = [
        load(conv_hbm, conv_ref, 2 * micro + 5),
        load(gain_hbm, gain_ref, 2 * micro + 6),
        load(cent_hbm, cent_ref, 2 * micro + 7),
        load(length_hbm, length_ref, 2 * micro + 8),
    ]
    grad_loads = [load(grad_hbm.at[m], grad_ref.at[m], m) for m in range(micro)]
    feat_loads = [load(feat_hbm.at[m], feat_ref.at[m], micro + m) for m in range(micro)]
    pre_load = load(preact_hbm, preact_ref, 2 * micro)
    out_load = load(w_out_hbm, w_out_ref, 2 * micro + 1)
    in_load = load(w_in_hbm, w_in_ref, 2 * micro + 2)
    for copy in (routed_load, slot_load, *grad_loads):
        copy.start()
    lax.fori_loop(1, n, greet, 0)
    for copy in (*small_loads, *feat_loads, pre_load, out_load, in_load):
        copy.start()

    def cols(c):
        return pl.ds(c * LANES, LANES)

    def to_blocks(rows, dst):
        for c in range(chunks):
            turn_ref[pl.ds(c, slots, stride=chunks), :] = rows[:, c * LANES : (c + 1) * LANES]
        dst[...] = turn_ref[...].astype(jnp.bfloat16).reshape(dst.shape)

    def from_blocks(src):
        turn_ref[...] = src[...].reshape(turn_ref.shape).astype(jnp.float32)
        for c in range(chunks):
            rows_ref[:, cols(c)] = turn_ref[pl.ds(c, slots, stride=chunks), :].astype(jnp.bfloat16)

    def exchange(src, dst, sent, got):
        def post(step, carry):
            peer = lax.rem(me + step * stride, n)
            pltpu.make_async_remote_copy(
                src_ref=src.at[peer],
                dst_ref=dst.at[me],
                send_sem=sent,
                recv_sem=got,
                device_id={axis: peer},
                device_id_type=MESH,
            ).start()
            return carry

        lax.fori_loop(1, n, post, 0)
        pltpu.make_async_copy(src.at[me], dst.at[me], got).start()

    def arrived(dst, got):
        pltpu.make_async_copy(dst, dst, got).wait()

    def departed(src, sent):
        part = src.at[pl.ds(0, n - 1)]
        pltpu.make_async_copy(part, part, sent).wait()

    routed_load.wait()
    slot_load.wait()
    for m in range(micro):
        grad_loads[m].wait()
        target = routed_ref[m : m + 1, :] * slot_cap + slot_ref[m : m + 1, :]
        onehot = (lax.broadcasted_iota(jnp.int32, (slots, frames), 0) == target).astype(
            jnp.float32
        ).astype(jnp.bfloat16)
        bucket = jnp.dot(onehot, grad_ref[m], preferred_element_type=jnp.float32)
        to_blocks(bucket, send_ref.at[m])
        if m == 0:
            pl.semaphore_wait(barrier, n - 1)
        exchange(send_ref.at[m], recv_ref.at[m], send_sem.at[m], recv_sem.at[m])

    for copy in small_loads:
        copy.wait()

    for c in range(chunks):
        taps_ref[c] = conv_ref[:, cols(c)].astype(jnp.float32)
        gain_f[c] = gain_ref[:, cols(c)].astype(jnp.float32)
        pad_ref[c, 0:low, :] = jnp.zeros((low, LANES), jnp.float32)
        pad_ref[c, low + frames :, :] = jnp.zeros((tap_count - low, LANES), jnp.float32)

    frame_at = lax.broadcasted_iota(jnp.int32, (frames, 1), 0)

    masks, inv_all, gate_all, exp_all, slot_all, slot_hot = [], [], [], [], [], []
    for m in range(micro):
        feat_loads[m].wait()
        mask = (frame_at < length_ref[0, m]).astype(jnp.float32)
        routed = to_column(routed_ref[m : m + 1, :])
        slot_pos = to_column(slot_ref[m : m + 1, :])
        exp_hot = (
            lax.broadcasted_iota(jnp.int32, (frames, experts), 1) == routed
        ).astype(jnp.float32)
        cent_rows[m] = jnp.dot(
            exp_hot.astype(jnp.bfloat16), cent_ref[...], preferred_element_type=jnp.float32
        ).astype(jnp.bfloat16)

        def ahead(c, square):
            lanes = pl.ds(pl.multiple_of(c * LANES, LANES), LANES)
            feats = feat_ref[m, :, lanes].astype(jnp.float32)
            pad_ref[c, low : low + frames, :] = feats * mask
            acc = jnp.zeros((frames, LANES), jnp.float32)
            for k in range(tap_count):
                acc = acc + taps_ref[c, k : k + 1, :] * pad_ref[c, k : k + frames, :]
            sig = jax.nn.sigmoid(acc)
            resid = feats + mask * acc * sig
            resid_ref[m, c] = resid
            slope_ref[m, c] = mask * sig * (1.0 + acc * (1.0 - sig))
            return square + resid * resid

        square = lax.fori_loop(0, chunks, ahead, jnp.zeros((frames, LANES), jnp.float32))
        inv_rms = lax.rsqrt(jnp.sum(square, axis=1, keepdims=True) * (1.0 / width) + 1e-06)

        def scoring(c, total):
            lanes = pl.ds(pl.multiple_of(c * LANES, LANES), LANES)
            normed = (resid_ref[m, c] * inv_rms * gain_f[c]).astype(jnp.bfloat16)
            return total + normed.astype(jnp.float32) * cent_rows[m, :, lanes].astype(jnp.float32)

        score = lax.fori_loop(0, chunks, scoring, jnp.zeros((frames, LANES), jnp.float32))
        gate_all.append(jax.nn.sigmoid(jnp.sum(score, axis=1, keepdims=True)))
        masks.append(mask)
        inv_all.append(inv_rms)
        exp_all.append(exp_hot)
        slot_all.append(slot_pos)
        slot_hot.append(
            (
                lax.broadcasted_iota(jnp.int32, (frames, slots), 1)
                == routed * slot_cap + slot_pos
            ).astype(jnp.float32).astype(jnp.bfloat16)
        )

        if m == 0:
            pre_load.wait()
        act = preact_ref[m].astype(jnp.float32)
        cdf = 0.5 * (1.0 + lax.erf(act * (1.0 / math.sqrt(2.0))))
        gelu_ref[m] = act * cdf
        gelu_slope_ref[m] = cdf + act * jnp.exp(-0.5 * act * act) * (
            1.0 / math.sqrt(2.0 * math.pi)
        )

    out_load.wait()
    in_load.wait()
    slot_id = lax.broadcasted_iota(jnp.int32, (slots, LANES), 0)
    lane_id = lax.broadcasted_iota(jnp.int32, (slots, LANES), 1)
    group_first = lax.broadcasted_iota(jnp.int32, (n, slots), 0) * slot_cap
    group_slot = lax.broadcasted_iota(jnp.int32, (n, slots), 1)
    grouped = jnp.logical_and(
        group_slot >= group_first, group_slot < group_first + slot_cap
    ).astype(jnp.float32)
    for m in range(micro):
        arrived(recv_ref.at[m], recv_sem.at[m])
        from_blocks(recv_ref.at[m])
        hidden = contract_last(rows_ref[...], w_out_ref[...])
        gate = jnp.sum(hidden * gelu_ref[m], axis=1, keepdims=True)
        pre_grad = (hidden * gelu_slope_ref[m]).astype(jnp.bfloat16)
        spread = jnp.where(lax.rem(slot_id, slot_cap) == lane_id, gate, 0.0)
        gate_rows = jnp.dot(
            grouped, spread, preferred_element_type=jnp.float32, precision=lax.Precision.HIGHEST
        )
        gate_send[m] = gate_rows.reshape(gate_send.shape[1:])
        exchange(gate_send.at[m], gate_recv.at[m], gate_send_sem.at[m], gate_recv_sem.at[m])
        to_blocks(contract_last(pre_grad, w_in_ref[...]), back_ref.at[m])
        exchange(back_ref.at[m], home_ref.at[m], back_sem.at[m], home_sem.at[m])

    frame_lane = lax.broadcasted_iota(jnp.int32, (frames, LANES), 1)
    for m in range(micro):
        mask, inv_rms, gate_val = masks[m], inv_all[m], gate_all[m]
        arrived(gate_recv.at[m], gate_recv_sem.at[m])
        picked = jnp.dot(
            exp_all[m],
            gate_recv[m].reshape(n, LANES),
            preferred_element_type=jnp.float32,
            precision=lax.Precision.HIGHEST,
        )
        gate_grad = jnp.sum(
            jnp.where(frame_lane == slot_all[m], picked, 0.0),
            axis=1,
            keepdims=True,
        )
        cent_scale = gate_val * (1.0 - gate_val) * gate_grad
        arrived(home_ref.at[m], home_sem.at[m])
        from_blocks(home_ref.at[m])
        slot_back[...] = jnp.dot(slot_hot[m], rows_ref[...], preferred_element_type=jnp.float32)

        def scaling(c, total):
            lanes = pl.ds(pl.multiple_of(c * LANES, LANES), LANES)
            grad = gate_val * slot_back[:, lanes] + cent_scale * cent_rows[m, :, lanes].astype(
                jnp.float32
            )
            scaled = grad * gain_f[c]
            slot_back[:, lanes] = scaled
            return total + resid_ref[m, c] * scaled

        total = lax.fori_loop(0, chunks, scaling, jnp.zeros((frames, LANES), jnp.float32))
        mean = jnp.sum(total, axis=1, keepdims=True) * (1.0 / width)
        back_scale = inv_rms * inv_rms * inv_rms * mean

        def finish(c, carry):
            lanes = pl.ds(pl.multiple_of(c * LANES, LANES), LANES)
            resid_grad = (
                grad_ref[m, :, lanes].astype(jnp.float32)
                + inv_rms * slot_back[:, lanes]
                - resid_ref[m, c] * back_scale
            )
            pad_ref[c, low : low + frames, :] = slope_ref[m, c] * resid_grad
            acc = jnp.zeros((frames, LANES), jnp.float32)
            for k in range(tap_count):
                first = 2 * low - k
                acc = acc + taps_ref[c, k : k + 1, :] * pad_ref[c, first : first + frames, :]
            out_ref[m, :, lanes] = (resid_grad + mask * acc).astype(jnp.bfloat16)
            return carry

        lax.fori_loop(0, chunks, finish, 0)
        pltpu.make_async_copy(out_ref.at[m], out_hbm.at[m], out_sem.at[m]).start()

    for m in range(micro):
        departed(send_ref.at[m], send_sem.at[m])
        departed(back_ref.at[m], back_sem.at[m])
        departed(gate_send.at[m], gate_send_sem.at[m])
    for m in range(micro):
        pltpu.make_async_copy(out_ref.at[m], out_hbm.at[m], out_sem.at[m]).wait()


def block_grads(
    grads, feats, lengths, routed, slot_pos, preact, conv_k, gain, cent, weight_in, weight_out
):
    micro, frames, width = feats.shape
    n = lax.axis_size("expert")
    hidden = weight_in.shape[1]
    cap = preact.shape[1] // n
    whole_rows = 16 * LANES // math.gcd(16 * LANES, width)
    slot_cap = -(-cap // whole_rows) * whole_rows
    if slot_cap != cap:
        preact = jnp.pad(
            preact.reshape(micro, n, cap, hidden), ((0, 0), (0, 0), (0, slot_cap - cap), (0, 0))
        ).reshape(micro, n * slot_cap, hidden)
    slots = n * slot_cap
    chunks = width // LANES
    taps = conv_k.shape[0]
    block = (n, slot_cap * chunks, LANES)
    bf16, f32 = jnp.bfloat16, jnp.float32
    in_hbm = pl.BlockSpec(memory_space=pltpu.HBM)
    anywhere = pl.BlockSpec(memory_space=pl.ANY)
    dma = pltpu.SemaphoreType.DMA
    flops = micro * (4 * slots * width * hidden + 4 * frames * width * (taps + slots))
    return pl.pallas_call(
        functools.partial(kernel, "expert", n, slot_cap),
        out_shape=jax.ShapeDtypeStruct((micro, frames, width), bf16),
        in_specs=[in_hbm] * 11,
        out_specs=anywhere,
        scratch_shapes=[
            pltpu.SMEM((1, micro), jnp.int32),
            pltpu.VMEM((micro, frames), jnp.int32),
            pltpu.VMEM((micro, frames), jnp.int32),
            pltpu.VMEM((taps, width), bf16),
            pltpu.VMEM((1, width), bf16),
            pltpu.VMEM((n, width), bf16),
            pltpu.VMEM((micro, frames, width), bf16),
            pltpu.VMEM((micro, frames, width), bf16),
            pltpu.VMEM((micro, slots, hidden), bf16),
            pltpu.VMEM((width, hidden), bf16),
            pltpu.VMEM((hidden, width), bf16),
            pltpu.VMEM((micro, frames, width), bf16),
            pltpu.VMEM((chunks, taps, LANES), f32),
            pltpu.VMEM((chunks, 1, LANES), f32),
            pltpu.VMEM((micro, *block), bf16),
            pltpu.VMEM((micro, *block), bf16),
            pltpu.VMEM((micro, *block), bf16),
            pltpu.VMEM((micro, *block), bf16),
            pltpu.VMEM((micro, n, 1, LANES), f32),
            pltpu.VMEM((micro, n, 1, LANES), f32),
            pltpu.VMEM((slots * chunks, LANES), f32),
            pltpu.VMEM((slots, width), bf16),
            pltpu.VMEM((chunks, frames + taps, LANES), f32),
            pltpu.VMEM((micro, chunks, frames, LANES), f32),
            pltpu.VMEM((micro, chunks, frames, LANES), f32),
            pltpu.VMEM((micro, frames, width), bf16),
            pltpu.VMEM((micro, slots, hidden), f32),
            pltpu.VMEM((micro, slots, hidden), f32),
            pltpu.VMEM((frames, width), f32),
            dma((2 * micro + 9,)),
            dma((micro,)),
            dma((micro,)),
            dma((micro,)),
            dma((micro,)),
            dma((micro,)),
            dma((micro,)),
            dma((micro,)),
        ],
        compiler_params=pltpu.CompilerParams(
            collective_id=0, has_side_effects=True, vmem_limit_bytes=60 * 1024 * 1024
        ),
        cost_estimate=pl.CostEstimate(
            flops=flops, bytes_accessed=8 * 1024 * 1024, transcendentals=0
        ),
    )(lengths.reshape(1, micro), routed, slot_pos, conv_k, gain, cent, feats, grads, preact, weight_in, weight_out)


def on_device(
    feat_saved,
    out_grad,
    lengths,
    expert_ids,
    slot_ids,
    expert_preact,
    conv_weight,
    norm_gain,
    centroids,
    w_in,
    w_out,
):
    section_count = lax.axis_size("section")
    micro_count = out_grad.shape[0]
    feats, routed, slots, preact = feat_saved[0], expert_ids[0], slot_ids[0], expert_preact[0]
    fixed = (conv_weight[0], norm_gain, centroids[0], w_in[0, 0], w_out[0, 0])
    if section_count == 1:
        return block_grads(out_grad, feats, lengths, routed, slots, preact, *fixed)[None]

    section_idx = lax.axis_index("section")
    route = [(i + 1, i) for i in range(section_count - 1)]

    def one_tick(tick_idx, carry):
        incoming, grads = carry
        micro_pos = tick_idx - (section_count - 1 - section_idx)
        is_valid = jnp.logical_and(micro_pos >= 0, micro_pos < micro_count)
        micro_sel = jnp.clip(micro_pos, 0, micro_count - 1)

        def pick(array):
            return lax.dynamic_slice_in_dim(array, micro_sel, 1, 0)

        grad_in = jnp.where(section_idx == section_count - 1, pick(out_grad), incoming)
        new_grad = block_grads(
            grad_in, pick(feats), pick(lengths), pick(routed), pick(slots), pick(preact), *fixed
        )
        updated = lax.dynamic_update_slice_in_dim(grads, new_grad, micro_sel, 0)
        grads = jnp.where(is_valid, updated, grads)
        return (lax.ppermute(new_grad, "section", route), grads)

    start = (jnp.zeros((1, *out_grad.shape[1:]), jnp.bfloat16), jnp.zeros_like(out_grad))
    _, grads = lax.fori_loop(0, section_count + micro_count - 1, one_tick, start)
    return grads[None]


def solution(mesh):
    in_specs = (
        P("section", None, "expert", None),
        P(None, "expert", None),
        P(None, "expert"),
        P("section", None, "expert"),
        P("section", None, "expert"),
        P("section", None, "expert", None),
        P("section", None, None),
        P("section", None),
        P("section", None, None),
        P("section", "expert", None, None),
        P("section", "expert", None, None),
    )
    out_specs = P("section", None, "expert", None)
    return jax.shard_map(
        on_device, mesh=mesh, in_specs=in_specs, out_specs=out_specs, check_vma=False
    )
```

```python
import functools
import math

import jax
import jax.numpy as jnp
from jax import lax
from jax.experimental import pallas as pl
from jax.experimental.pallas import tpu as pltpu
from jax.sharding import PartitionSpec as P

LANES = 128
SUB = 8
MESH = pl.DeviceIdType.MESH


def contract_last(left, right):
    return lax.dot_general(
        left, right, (((1,), (1,)), ((), ())), preferred_element_type=jnp.float32
    )


def to_column(row):
    size = row.shape[1]
    same = lax.broadcasted_iota(jnp.int32, (size, size), 0) == lax.broadcasted_iota(
        jnp.int32, (size, size), 1
    )
    wide = jnp.broadcast_to(row.astype(jnp.float32), (size, size))
    return jnp.sum(jnp.where(same, wide, 0.0), axis=1, keepdims=True).astype(jnp.int32)


def kernel(
    axis,
    n,
    slot_cap,
    length_hbm,
    routed_hbm,
    slot_hbm,
    conv_hbm,
    gain_hbm,
    cent_hbm,
    feat_hbm,
    grad_hbm,
    preact_hbm,
    w_in_hbm,
    w_out_hbm,
    out_hbm,
    length_ref,
    routed_ref,
    slot_ref,
    conv_ref,
    gain_ref,
    cent_ref,
    feat_ref,
    grad_ref,
    preact_ref,
    w_in_ref,
    w_out_ref,
    out_ref,
    taps_ref,
    gain_f,
    send_ref,
    recv_ref,
    back_ref,
    home_ref,
    gate_send,
    gate_recv,
    turn_ref,
    rows_ref,
    pad_ref,
    resid_ref,
    slope_ref,
    cent_rows,
    gelu_ref,
    gelu_slope_ref,
    slot_back,
    load_sem,
    out_sem,
    send_sem,
    recv_sem,
    back_sem,
    home_sem,
    gate_send_sem,
    gate_recv_sem,
):
    micro, frames, width = feat_ref.shape
    stride = next(k for k in range(n // 3 + 1, 2 * n) if math.gcd(k, n) == 1)
    chunks = width // LANES
    slots = n * slot_cap
    tap_count = conv_ref.shape[0]
    low = tap_count // 2
    experts = n
    me = lax.axis_index(axis)

    barrier = pltpu.get_barrier_semaphore()

    def greet(step, carry):
        pl.semaphore_signal(
            barrier, inc=1, device_id={axis: lax.rem(me + step, n)}, device_id_type=MESH
        )
        return carry

    def load(src, dst, at):
        return pltpu.make_async_copy(src, dst, load_sem.at[at])

    routed_load = load(routed_hbm, routed_ref, 2 * micro + 3)
    slot_load = load(slot_hbm, slot_ref, 2 * micro + 4)
    small_loads = [
        load(conv_hbm, conv_ref, 2 * micro + 5),
        load(gain_hbm, gain_ref, 2 * micro + 6),
        load(cent_hbm, cent_ref, 2 * micro + 7),
        load(length_hbm, length_ref, 2 * micro + 8),
    ]
    grad_loads = [load(grad_hbm.at[m], grad_ref.at[m], m) for m in range(micro)]
    feat_loads = [load(feat_hbm.at[m], feat_ref.at[m], micro + m) for m in range(micro)]
    pre_load = load(preact_hbm, preact_ref, 2 * micro)
    out_load = load(w_out_hbm, w_out_ref, 2 * micro + 1)
    in_load = load(w_in_hbm, w_in_ref, 2 * micro + 2)
    for copy in (routed_load, slot_load, *grad_loads):
        copy.start()
    lax.fori_loop(1, n, greet, 0)
    for copy in (*small_loads, *feat_loads, pre_load, out_load, in_load):
        copy.start()

    def cols(c):
        return pl.ds(c * LANES, LANES)

    def to_blocks(rows, dst):
        for c in range(chunks):
            turn_ref[pl.ds(c, slots, stride=chunks), :] = rows[:, c * LANES : (c + 1) * LANES]
        dst[...] = turn_ref[...].astype(jnp.bfloat16).reshape(dst.shape)

    def from_blocks(src):
        turn_ref[...] = src[...].reshape(turn_ref.shape).astype(jnp.float32)
        for c in range(chunks):
            rows_ref[:, cols(c)] = turn_ref[pl.ds(c, slots, stride=chunks), :].astype(jnp.bfloat16)

    def exchange(src, dst, sent, got):
        def post(step, carry):
            peer = lax.rem(me + step * stride, n)
            pltpu.make_async_remote_copy(
                src_ref=src.at[peer],
                dst_ref=dst.at[me],
                send_sem=sent,
                recv_sem=got,
                device_id={axis: peer},
                device_id_type=MESH,
            ).start()
            return carry

        lax.fori_loop(1, n, post, 0)
        pltpu.make_async_copy(src.at[me], dst.at[me], got).start()

    def arrived(dst, got):
        pltpu.make_async_copy(dst, dst, got).wait()

    def departed(src, sent):
        part = src.at[pl.ds(0, n - 1)]
        pltpu.make_async_copy(part, part, sent).wait()

    def dispatch(m):
        exchange(send_ref.at[m], recv_ref.at[m], send_sem.at[m], recv_sem.at[m])

    routed_load.wait()
    slot_load.wait()
    for m in range(micro):
        grad_loads[m].wait()
        target = routed_ref[m : m + 1, :] * slot_cap + slot_ref[m : m + 1, :]
        onehot = (lax.broadcasted_iota(jnp.int32, (slots, frames), 0) == target).astype(
            jnp.float32
        ).astype(jnp.bfloat16)
        bucket = jnp.dot(onehot, grad_ref[m], preferred_element_type=jnp.float32)
        to_blocks(bucket, send_ref.at[m])
        if m == 0:
            pl.semaphore_wait(barrier, n - 1)
            dispatch(m)

    for copy in small_loads:
        copy.wait()

    for c in range(chunks):
        taps_ref[c] = conv_ref[:, cols(c)].astype(jnp.float32)
        gain_f[c] = gain_ref[:, cols(c)].astype(jnp.float32)
        pad_ref[c, 0:low, :] = jnp.zeros((low, LANES), jnp.float32)
        pad_ref[c, low + frames :, :] = jnp.zeros((tap_count - low, LANES), jnp.float32)

    def conv(c, start, tap_of):
        acc = jnp.zeros((frames, LANES), jnp.float32)
        reach = (tap_count - 1) // SUB * SUB
        for offset in range(start, start + SUB):
            rows = pad_ref[c, offset : offset + frames + reach, :]
            for first in range(0, reach + 1, SUB):
                k = tap_of(offset + first)
                acc = acc + taps_ref[c, k : k + 1, :] * rows[first : first + frames, :]
        return acc

    frame_at = lax.broadcasted_iota(jnp.int32, (frames, 1), 0)

    masks, inv_all, gate_all, exp_all, slot_all, slot_hot = [], [], [], [], [], []
    for m in range(micro):
        feat_loads[m].wait()
        mask = (frame_at < length_ref[0, m]).astype(jnp.float32)
        routed = to_column(routed_ref[m : m + 1, :])
        slot_pos = to_column(slot_ref[m : m + 1, :])
        exp_hot = (
            lax.broadcasted_iota(jnp.int32, (frames, experts), 1) == routed
        ).astype(jnp.float32)
        cent_rows[m] = jnp.dot(
            exp_hot.astype(jnp.bfloat16), cent_ref[...], preferred_element_type=jnp.float32
        ).astype(jnp.bfloat16)

        def ahead(c, square):
            lanes = pl.ds(pl.multiple_of(c * LANES, LANES), LANES)
            feats = feat_ref[m, :, lanes].astype(jnp.float32)
            pad_ref[c, low : low + frames, :] = feats * mask
            acc = conv(c, 0, lambda first: first)
            sig = jax.nn.sigmoid(acc)
            resid = feats + mask * acc * sig
            resid_ref[m, c] = resid
            slope_ref[m, c] = mask * sig * (1.0 + acc * (1.0 - sig))
            return square + resid * resid

        square = lax.fori_loop(0, chunks, ahead, jnp.zeros((frames, LANES), jnp.float32))
        if m + 1 < micro:
            dispatch(m + 1)
        inv_rms = lax.rsqrt(jnp.sum(square, axis=1, keepdims=True) * (1.0 / width) + 1e-06)

        def scoring(c, total):
            lanes = pl.ds(pl.multiple_of(c * LANES, LANES), LANES)
            normed = (resid_ref[m, c] * inv_rms * gain_f[c]).astype(jnp.bfloat16)
            return total + normed.astype(jnp.float32) * cent_rows[m, :, lanes].astype(jnp.float32)

        score = lax.fori_loop(0, chunks, scoring, jnp.zeros((frames, LANES), jnp.float32))
        gate_all.append(jax.nn.sigmoid(jnp.sum(score, axis=1, keepdims=True)))
        masks.append(mask)
        inv_all.append(inv_rms)
        exp_all.append(exp_hot)
        slot_all.append(slot_pos)
        slot_hot.append(
            (
                lax.broadcasted_iota(jnp.int32, (frames, slots), 1)
                == routed * slot_cap + slot_pos
            ).astype(jnp.float32).astype(jnp.bfloat16)
        )

        if m == 0:
            pre_load.wait()
        act = preact_ref[m].astype(jnp.float32)
        cdf = 0.5 * (1.0 + lax.erf(act * (1.0 / math.sqrt(2.0))))
        gelu_ref[m] = act * cdf
        gelu_slope_ref[m] = cdf + act * jnp.exp(-0.5 * act * act) * (
            1.0 / math.sqrt(2.0 * math.pi)
        )

    out_load.wait()
    in_load.wait()
    slot_id = lax.broadcasted_iota(jnp.int32, (slots, LANES), 0)
    lane_id = lax.broadcasted_iota(jnp.int32, (slots, LANES), 1)
    group_first = lax.broadcasted_iota(jnp.int32, (n, slots), 0) * slot_cap
    group_slot = lax.broadcasted_iota(jnp.int32, (n, slots), 1)
    grouped = jnp.logical_and(
        group_slot >= group_first, group_slot < group_first + slot_cap
    ).astype(jnp.float32)
    for m in range(micro):
        arrived(recv_ref.at[m], recv_sem.at[m])
        from_blocks(recv_ref.at[m])
        hidden = contract_last(rows_ref[...], w_out_ref[...])
        gate = jnp.sum(hidden * gelu_ref[m], axis=1, keepdims=True)
        pre_grad = (hidden * gelu_slope_ref[m]).astype(jnp.bfloat16)
        spread = jnp.where(lax.rem(slot_id, slot_cap) == lane_id, gate, 0.0)
        gate_rows = jnp.dot(
            grouped, spread, preferred_element_type=jnp.float32, precision=lax.Precision.HIGHEST
        )
        gate_send[m] = gate_rows.reshape(gate_send.shape[1:])
        exchange(gate_send.at[m], gate_recv.at[m], gate_send_sem.at[m], gate_recv_sem.at[m])
        to_blocks(contract_last(pre_grad, w_in_ref[...]), back_ref.at[m])
        exchange(back_ref.at[m], home_ref.at[m], back_sem.at[m], home_sem.at[m])

    frame_lane = lax.broadcasted_iota(jnp.int32, (frames, LANES), 1)
    for m in range(micro):
        mask, inv_rms, gate_val = masks[m], inv_all[m], gate_all[m]
        arrived(gate_recv.at[m], gate_recv_sem.at[m])
        picked = jnp.dot(
            exp_all[m],
            gate_recv[m].reshape(n, LANES),
            preferred_element_type=jnp.float32,
            precision=lax.Precision.HIGHEST,
        )
        gate_grad = jnp.sum(
            jnp.where(frame_lane == slot_all[m], picked, 0.0),
            axis=1,
            keepdims=True,
        )
        cent_scale = gate_val * (1.0 - gate_val) * gate_grad
        arrived(home_ref.at[m], home_sem.at[m])
        from_blocks(home_ref.at[m])
        slot_back[...] = jnp.dot(slot_hot[m], rows_ref[...], preferred_element_type=jnp.float32)

        def scaling(c, total):
            lanes = pl.ds(pl.multiple_of(c * LANES, LANES), LANES)
            grad = gate_val * slot_back[:, lanes] + cent_scale * cent_rows[m, :, lanes].astype(
                jnp.float32
            )
            scaled = grad * gain_f[c]
            slot_back[:, lanes] = scaled
            return total + resid_ref[m, c] * scaled

        total = lax.fori_loop(0, chunks, scaling, jnp.zeros((frames, LANES), jnp.float32))
        mean = jnp.sum(total, axis=1, keepdims=True) * (1.0 / width)
        back_scale = inv_rms * inv_rms * inv_rms * mean

        def finish(c, carry):
            lanes = pl.ds(pl.multiple_of(c * LANES, LANES), LANES)
            resid_grad = (
                grad_ref[m, :, lanes].astype(jnp.float32)
                + inv_rms * slot_back[:, lanes]
                - resid_ref[m, c] * back_scale
            )
            pad_ref[c, low : low + frames, :] = slope_ref[m, c] * resid_grad
            acc = conv(c, 1, lambda first: 2 * low - first)
            out_ref[m, :, lanes] = (resid_grad + mask * acc).astype(jnp.bfloat16)
            return carry

        lax.fori_loop(0, chunks, finish, 0)
        pltpu.make_async_copy(out_ref.at[m], out_hbm.at[m], out_sem.at[m]).start()

    for m in range(micro):
        departed(send_ref.at[m], send_sem.at[m])
        departed(back_ref.at[m], back_sem.at[m])
        departed(gate_send.at[m], gate_send_sem.at[m])
    for m in range(micro):
        pltpu.make_async_copy(out_ref.at[m], out_hbm.at[m], out_sem.at[m]).wait()


def hand_over(pieces, src, dst, sem):
    micro, frames, _ = src.shape
    part = frames // pieces
    copies = [
        pltpu.make_async_copy(
            src.at[m, pl.ds(i * part, part)], dst.at[m, pl.ds(i * part, part)], sem.at[m, i]
        )
        for m in range(micro)
        for i in range(pieces)
    ]
    for copy in copies:
        copy.start()
    for copy in copies:
        copy.wait()


def block_grads(
    grads, feats, lengths, routed, slot_pos, preact, conv_k, gain, cent, weight_in, weight_out
):
    micro, frames, width = feats.shape
    n = lax.axis_size("expert")
    hidden = weight_in.shape[1]
    cap = preact.shape[1] // n
    whole_rows = 16 * LANES // math.gcd(16 * LANES, width)
    slot_cap = -(-cap // whole_rows) * whole_rows
    if slot_cap != cap:
        preact = jnp.pad(
            preact.reshape(micro, n, cap, hidden), ((0, 0), (0, 0), (0, slot_cap - cap), (0, 0))
        ).reshape(micro, n * slot_cap, hidden)
    slots = n * slot_cap
    chunks = width // LANES
    taps = conv_k.shape[0]
    block = (n, slot_cap * chunks, LANES)
    bf16, f32 = jnp.bfloat16, jnp.float32
    in_hbm = pl.BlockSpec(memory_space=pltpu.HBM)
    anywhere = pl.BlockSpec(memory_space=pl.ANY)
    dma = pltpu.SemaphoreType.DMA
    flops = micro * (4 * slots * width * hidden + 4 * frames * width * (taps + slots))
    result = pl.pallas_call(
        functools.partial(kernel, "expert", n, slot_cap),
        out_shape=jax.ShapeDtypeStruct((micro, frames, width), bf16),
        in_specs=[in_hbm] * 11,
        out_specs=anywhere,
        scratch_shapes=[
            pltpu.SMEM((1, micro), jnp.int32),
            pltpu.VMEM((micro, frames), jnp.int32),
            pltpu.VMEM((micro, frames), jnp.int32),
            pltpu.VMEM((taps, width), bf16),
            pltpu.VMEM((1, width), bf16),
            pltpu.VMEM((n, width), bf16),
            pltpu.VMEM((micro, frames, width), bf16),
            pltpu.VMEM((micro, frames, width), bf16),
            pltpu.VMEM((micro, slots, hidden), bf16),
            pltpu.VMEM((width, hidden), bf16),
            pltpu.VMEM((hidden, width), bf16),
            pltpu.VMEM((micro, frames, width), bf16),
            pltpu.VMEM((chunks, taps, LANES), f32),
            pltpu.VMEM((chunks, 1, LANES), f32),
            pltpu.VMEM((micro, *block), bf16),
            pltpu.VMEM((micro, *block), bf16),
            pltpu.VMEM((micro, *block), bf16),
            pltpu.VMEM((micro, *block), bf16),
            pltpu.VMEM((micro, n, 1, LANES), f32),
            pltpu.VMEM((micro, n, 1, LANES), f32),
            pltpu.VMEM((slots * chunks, LANES), f32),
            pltpu.VMEM((slots, width), bf16),
            pltpu.VMEM((chunks, frames + taps, LANES), f32),
            pltpu.VMEM((micro, chunks, frames, LANES), f32),
            pltpu.VMEM((micro, chunks, frames, LANES), f32),
            pltpu.VMEM((micro, frames, width), bf16),
            pltpu.VMEM((micro, slots, hidden), f32),
            pltpu.VMEM((micro, slots, hidden), f32),
            pltpu.VMEM((frames, width), f32),
            dma((2 * micro + 9,)),
            dma((micro,)),
            dma((micro,)),
            dma((micro,)),
            dma((micro,)),
            dma((micro,)),
            dma((micro,)),
            dma((micro,)),
        ],
        compiler_params=pltpu.CompilerParams(
            collective_id=0, has_side_effects=True, vmem_limit_bytes=60 * 1024 * 1024
        ),
        cost_estimate=pl.CostEstimate(
            flops=flops, bytes_accessed=8 * 1024 * 1024, transcendentals=0
        ),
    )(lengths.reshape(1, micro), routed, slot_pos, conv_k, gain, cent, feats, grads, preact, weight_in, weight_out)
    pieces = 4
    return pl.pallas_call(
        functools.partial(hand_over, pieces),
        out_shape=jax.ShapeDtypeStruct(result.shape, result.dtype),
        in_specs=[anywhere],
        out_specs=anywhere,
        scratch_shapes=[dma((micro, pieces))],
        compiler_params=pltpu.CompilerParams(vmem_limit_bytes=60 * 1024 * 1024),
    )(result)


def on_device(
    feat_saved,
    out_grad,
    lengths,
    expert_ids,
    slot_ids,
    expert_preact,
    conv_weight,
    norm_gain,
    centroids,
    w_in,
    w_out,
):
    section_count = lax.axis_size("section")
    micro_count = out_grad.shape[0]
    feats, routed, slots, preact = feat_saved[0], expert_ids[0], slot_ids[0], expert_preact[0]
    fixed = (conv_weight[0], norm_gain, centroids[0], w_in[0, 0], w_out[0, 0])
    if section_count == 1:
        return block_grads(out_grad, feats, lengths, routed, slots, preact, *fixed)[None]

    section_idx = lax.axis_index("section")
    route = [(i + 1, i) for i in range(section_count - 1)]

    def one_tick(tick_idx, carry):
        incoming, grads = carry
        micro_pos = tick_idx - (section_count - 1 - section_idx)
        is_valid = jnp.logical_and(micro_pos >= 0, micro_pos < micro_count)
        micro_sel = jnp.clip(micro_pos, 0, micro_count - 1)

        def pick(array):
            return lax.dynamic_slice_in_dim(array, micro_sel, 1, 0)

        grad_in = jnp.where(section_idx == section_count - 1, pick(out_grad), incoming)
        new_grad = block_grads(
            grad_in, pick(feats), pick(lengths), pick(routed), pick(slots), pick(preact), *fixed
        )
        updated = lax.dynamic_update_slice_in_dim(grads, new_grad, micro_sel, 0)
        grads = jnp.where(is_valid, updated, grads)
        return (lax.ppermute(new_grad, "section", route), grads)

    start = (jnp.zeros((1, *out_grad.shape[1:]), jnp.bfloat16), jnp.zeros_like(out_grad))
    _, grads = lax.fori_loop(0, section_count + micro_count - 1, one_tick, start)
    return grads[None]


def solution(mesh):
    in_specs = (
        P("section", None, "expert", None),
        P(None, "expert", None),
        P(None, "expert"),
        P("section", None, "expert"),
        P("section", None, "expert"),
        P("section", None, "expert", None),
        P("section", None, None),
        P("section", None),
        P("section", None, None),
        P("section", "expert", None, None),
        P("section", "expert", None, None),
    )
    out_specs = P("section", None, "expert", None)
    return jax.shard_map(
        on_device, mesh=mesh, in_specs=in_specs, out_specs=out_specs, check_vma=False
    )
```

```python
import functools
import math

import jax
import jax.numpy as jnp
from jax import lax
from jax.experimental import pallas as pl
from jax.experimental.pallas import tpu as pltpu
from jax.sharding import PartitionSpec as P

LANES = 128
SUB = 8
MESH = pl.DeviceIdType.MESH


def contract_last(left, right):
    return lax.dot_general(
        left, right, (((1,), (1,)), ((), ())), preferred_element_type=jnp.float32
    )


def to_column(row):
    size = row.shape[1]
    same = lax.broadcasted_iota(jnp.int32, (size, size), 0) == lax.broadcasted_iota(
        jnp.int32, (size, size), 1
    )
    wide = jnp.broadcast_to(row.astype(jnp.float32), (size, size))
    return jnp.sum(jnp.where(same, wide, 0.0), axis=1, keepdims=True).astype(jnp.int32)


def kernel(
    axis,
    n,
    slot_cap,
    length_hbm,
    routed_hbm,
    slot_hbm,
    conv_hbm,
    gain_hbm,
    cent_hbm,
    feat_hbm,
    grad_hbm,
    preact_hbm,
    w_in_hbm,
    w_out_hbm,
    out_ref,
    length_ref,
    routed_ref,
    slot_ref,
    conv_ref,
    gain_ref,
    cent_ref,
    feat_ref,
    grad_ref,
    preact_ref,
    w_in_ref,
    w_out_ref,
    taps_ref,
    gain_f,
    send_ref,
    recv_ref,
    back_ref,
    home_ref,
    gate_send,
    gate_recv,
    turn_ref,
    rows_ref,
    pad_ref,
    resid_ref,
    slope_ref,
    cent_rows,
    gelu_ref,
    gelu_slope_ref,
    slot_back,
    load_sem,
    send_sem,
    recv_sem,
    back_sem,
    home_sem,
    gate_send_sem,
    gate_recv_sem,
):
    micro, frames, width = feat_ref.shape
    stride = next(k for k in range(n // 3 + 1, 2 * n) if math.gcd(k, n) == 1)
    chunks = width // LANES
    slots = n * slot_cap
    tap_count = conv_ref.shape[0]
    low = tap_count // 2
    experts = n
    gate_span = LANES // micro
    me = lax.axis_index(axis)

    barrier = pltpu.get_barrier_semaphore()

    def greet(step, carry):
        pl.semaphore_signal(
            barrier, inc=1, device_id={axis: lax.rem(me + step, n)}, device_id_type=MESH
        )
        return carry

    def load(src, dst, at):
        return pltpu.make_async_copy(src, dst, load_sem.at[at])

    routed_load = load(routed_hbm, routed_ref, 2 * micro + 3)
    slot_load = load(slot_hbm, slot_ref, 2 * micro + 4)
    small_loads = [
        load(conv_hbm, conv_ref, 2 * micro + 5),
        load(gain_hbm, gain_ref, 2 * micro + 6),
        load(cent_hbm, cent_ref, 2 * micro + 7),
        load(length_hbm, length_ref, 2 * micro + 8),
    ]
    grad_loads = [load(grad_hbm.at[m], grad_ref.at[m], m) for m in range(micro)]
    feat_loads = [load(feat_hbm.at[m], feat_ref.at[m], micro + m) for m in range(micro)]
    pre_load = load(preact_hbm, preact_ref, 2 * micro)
    out_load = load(w_out_hbm, w_out_ref, 2 * micro + 1)
    in_load = load(w_in_hbm, w_in_ref, 2 * micro + 2)
    for copy in (routed_load, slot_load, *grad_loads):
        copy.start()
    lax.fori_loop(1, n, greet, 0)
    for copy in (*small_loads, *feat_loads, pre_load, out_load, in_load):
        copy.start()

    def cols(c):
        return pl.ds(c * LANES, LANES)

    def to_blocks(rows, dst):
        for c in range(chunks):
            turn_ref[pl.ds(c, slots, stride=chunks), :] = rows[:, c * LANES : (c + 1) * LANES]
        dst[...] = turn_ref[...].astype(jnp.bfloat16).reshape(dst.shape)

    def from_blocks(src):
        turn_ref[...] = src[...].reshape(turn_ref.shape).astype(jnp.float32)
        for c in range(chunks):
            rows_ref[:, cols(c)] = turn_ref[pl.ds(c, slots, stride=chunks), :].astype(jnp.bfloat16)

    def exchange(src, dst, sent, got):
        def post(step, carry):
            peer = lax.rem(me + step * stride, n)
            pltpu.make_async_remote_copy(
                src_ref=src.at[peer],
                dst_ref=dst.at[me],
                send_sem=sent,
                recv_sem=got,
                device_id={axis: peer},
                device_id_type=MESH,
            ).start()
            return carry

        lax.fori_loop(1, n, post, 0)
        pltpu.make_async_copy(src.at[me], dst.at[me], got).start()

    def arrived(dst, got):
        pltpu.make_async_copy(dst, dst, got).wait()

    def departed(src, sent):
        part = src.at[pl.ds(0, n - 1)]
        pltpu.make_async_copy(part, part, sent).wait()

    def dispatch(m):
        exchange(send_ref.at[m], recv_ref.at[m], send_sem.at[m], recv_sem.at[m])

    routed_load.wait()
    slot_load.wait()
    for m in range(micro):
        grad_loads[m].wait()
        target = routed_ref[m : m + 1, :] * slot_cap + slot_ref[m : m + 1, :]
        onehot = (lax.broadcasted_iota(jnp.int32, (slots, frames), 0) == target).astype(
            jnp.float32
        ).astype(jnp.bfloat16)
        bucket = jnp.dot(onehot, grad_ref[m], preferred_element_type=jnp.float32)
        to_blocks(bucket, send_ref.at[m])
        if m == 0:
            pl.semaphore_wait(barrier, n - 1)
            dispatch(m)

    for copy in small_loads:
        copy.wait()

    for c in range(chunks):
        taps_ref[c] = conv_ref[:, cols(c)].astype(jnp.float32)
        gain_f[c] = gain_ref[:, cols(c)].astype(jnp.float32)
        pad_ref[c, 0:low, :] = jnp.zeros((low, LANES), jnp.float32)
        pad_ref[c, low + frames :, :] = jnp.zeros((tap_count - low, LANES), jnp.float32)

    def conv(c, start, tap_of):
        acc = jnp.zeros((frames, LANES), jnp.float32)
        reach = (tap_count - 1) // SUB * SUB
        for offset in range(start, start + SUB):
            rows = pad_ref[c, offset : offset + frames + reach, :]
            for first in range(0, reach + 1, SUB):
                k = tap_of(offset + first)
                acc = acc + taps_ref[c, k : k + 1, :] * rows[first : first + frames, :]
        return acc

    frame_at = lax.broadcasted_iota(jnp.int32, (frames, 1), 0)

    masks, inv_all, gate_all, exp_all, slot_all, slot_hot = [], [], [], [], [], []
    for m in range(micro):
        feat_loads[m].wait()
        mask = (frame_at < length_ref[0, m]).astype(jnp.float32)
        routed = to_column(routed_ref[m : m + 1, :])
        slot_pos = to_column(slot_ref[m : m + 1, :])
        exp_hot = (
            lax.broadcasted_iota(jnp.int32, (frames, experts), 1) == routed
        ).astype(jnp.float32)
        cent_rows[m] = jnp.dot(
            exp_hot.astype(jnp.bfloat16), cent_ref[...], preferred_element_type=jnp.float32
        ).astype(jnp.bfloat16)

        def ahead(c, square):
            lanes = pl.ds(pl.multiple_of(c * LANES, LANES), LANES)
            feats = feat_ref[m, :, lanes].astype(jnp.float32)
            pad_ref[c, low : low + frames, :] = feats * mask
            acc = conv(c, 0, lambda first: first)
            sig = jax.nn.sigmoid(acc)
            resid = feats + mask * acc * sig
            resid_ref[m, c] = resid
            slope_ref[m, c] = mask * sig * (1.0 + acc * (1.0 - sig))
            return square + resid * resid

        square = lax.fori_loop(0, chunks, ahead, jnp.zeros((frames, LANES), jnp.float32))
        if m + 1 < micro:
            dispatch(m + 1)
        inv_rms = lax.rsqrt(jnp.sum(square, axis=1, keepdims=True) * (1.0 / width) + 1e-06)

        def scoring(c, total):
            lanes = pl.ds(pl.multiple_of(c * LANES, LANES), LANES)
            normed = (resid_ref[m, c] * inv_rms * gain_f[c]).astype(jnp.bfloat16)
            return total + normed.astype(jnp.float32) * cent_rows[m, :, lanes].astype(jnp.float32)

        score = lax.fori_loop(0, chunks, scoring, jnp.zeros((frames, LANES), jnp.float32))
        gate_all.append(jax.nn.sigmoid(jnp.sum(score, axis=1, keepdims=True)))
        masks.append(mask)
        inv_all.append(inv_rms)
        exp_all.append(exp_hot)
        slot_all.append(slot_pos)
        slot_hot.append(
            (
                lax.broadcasted_iota(jnp.int32, (frames, slots), 1)
                == routed * slot_cap + slot_pos
            ).astype(jnp.float32).astype(jnp.bfloat16)
        )

        if m == 0:
            pre_load.wait()
        act = preact_ref[m].astype(jnp.float32)
        cdf = 0.5 * (1.0 + lax.erf(act * (1.0 / math.sqrt(2.0))))
        gelu_ref[m] = act * cdf
        gelu_slope_ref[m] = cdf + act * jnp.exp(-0.5 * act * act) * (
            1.0 / math.sqrt(2.0 * math.pi)
        )

    out_load.wait()
    in_load.wait()
    gate_rows = jnp.zeros((n, LANES), jnp.float32)
    slot_id = lax.broadcasted_iota(jnp.int32, (slots, LANES), 0)
    lane_id = lax.broadcasted_iota(jnp.int32, (slots, LANES), 1)
    group_first = lax.broadcasted_iota(jnp.int32, (n, slots), 0) * slot_cap
    group_slot = lax.broadcasted_iota(jnp.int32, (n, slots), 1)
    grouped = jnp.logical_and(
        group_slot >= group_first, group_slot < group_first + slot_cap
    ).astype(jnp.float32)
    for m in range(micro):
        arrived(recv_ref.at[m], recv_sem.at[m])
        from_blocks(recv_ref.at[m])
        hidden = contract_last(rows_ref[...], w_out_ref[...])
        gate = jnp.sum(hidden * gelu_ref[m], axis=1, keepdims=True)
        pre_grad = (hidden * gelu_slope_ref[m]).astype(jnp.bfloat16)
        spread = jnp.where(lax.rem(slot_id, slot_cap) + m * gate_span == lane_id, gate, 0.0)
        gate_rows = gate_rows + jnp.dot(
            grouped, spread, preferred_element_type=jnp.float32, precision=lax.Precision.HIGHEST
        )
        if m == micro - 1:
            gate_send[...] = gate_rows.reshape(gate_send.shape)
            exchange(gate_send, gate_recv, gate_send_sem, gate_recv_sem)
        to_blocks(contract_last(pre_grad, w_in_ref[...]), back_ref.at[m])
        exchange(back_ref.at[m], home_ref.at[m], back_sem.at[m], home_sem.at[m])

    arrived(gate_recv, gate_recv_sem)
    frame_lane = lax.broadcasted_iota(jnp.int32, (frames, LANES), 1)
    for m in range(micro):
        mask, inv_rms, gate_val = masks[m], inv_all[m], gate_all[m]
        picked = jnp.dot(
            exp_all[m],
            gate_recv[...].reshape(n, LANES),
            preferred_element_type=jnp.float32,
            precision=lax.Precision.HIGHEST,
        )
        gate_grad = jnp.sum(
            jnp.where(frame_lane == slot_all[m] + m * gate_span, picked, 0.0),
            axis=1,
            keepdims=True,
        )
        cent_scale = gate_val * (1.0 - gate_val) * gate_grad
        arrived(home_ref.at[m], home_sem.at[m])
        from_blocks(home_ref.at[m])
        slot_back[...] = jnp.dot(slot_hot[m], rows_ref[...], preferred_element_type=jnp.float32)

        def scaling(c, total):
            lanes = pl.ds(pl.multiple_of(c * LANES, LANES), LANES)
            grad = gate_val * slot_back[:, lanes] + cent_scale * cent_rows[m, :, lanes].astype(
                jnp.float32
            )
            scaled = grad * gain_f[c]
            slot_back[:, lanes] = scaled
            return total + resid_ref[m, c] * scaled

        total = lax.fori_loop(0, chunks, scaling, jnp.zeros((frames, LANES), jnp.float32))
        mean = jnp.sum(total, axis=1, keepdims=True) * (1.0 / width)
        back_scale = inv_rms * inv_rms * inv_rms * mean

        def finish(c, carry):
            lanes = pl.ds(pl.multiple_of(c * LANES, LANES), LANES)
            resid_grad = (
                grad_ref[m, :, lanes].astype(jnp.float32)
                + inv_rms * slot_back[:, lanes]
                - resid_ref[m, c] * back_scale
            )
            pad_ref[c, low : low + frames, :] = slope_ref[m, c] * resid_grad
            acc = conv(c, 1, lambda first: 2 * low - first)
            out_ref[m, :, lanes] = (resid_grad + mask * acc).astype(jnp.bfloat16)
            return carry

        lax.fori_loop(0, chunks, finish, 0)

    for m in range(micro):
        departed(send_ref.at[m], send_sem.at[m])
        departed(back_ref.at[m], back_sem.at[m])
    departed(gate_send, gate_send_sem)


def block_grads(
    grads, feats, lengths, routed, slot_pos, preact, conv_k, gain, cent, weight_in, weight_out
):
    micro, frames, width = feats.shape
    n = lax.axis_size("expert")
    hidden = weight_in.shape[1]
    cap = preact.shape[1] // n
    whole_rows = 16 * LANES // math.gcd(16 * LANES, width)
    slot_cap = -(-cap // whole_rows) * whole_rows
    if slot_cap != cap:
        preact = jnp.pad(
            preact.reshape(micro, n, cap, hidden), ((0, 0), (0, 0), (0, slot_cap - cap), (0, 0))
        ).reshape(micro, n * slot_cap, hidden)
    slots = n * slot_cap
    chunks = width // LANES
    taps = conv_k.shape[0]
    block = (n, slot_cap * chunks, LANES)
    bf16, f32 = jnp.bfloat16, jnp.float32
    lengths = lengths.reshape(1, micro)
    held = (
        lengths, routed, slot_pos, conv_k, gain, cent, feats, grads, preact, weight_in, weight_out
    )
    operands = [pltpu.with_memory_space_constraint(x, pltpu.HBM) for x in held]
    in_hbm = pl.BlockSpec(memory_space=pltpu.HBM)
    dma = pltpu.SemaphoreType.DMA
    flops = micro * (4 * slots * width * hidden + 4 * frames * width * (taps + slots))
    return pl.pallas_call(
        functools.partial(kernel, "expert", n, slot_cap),
        out_shape=jax.ShapeDtypeStruct((micro, frames, width), bf16),
        in_specs=[in_hbm] * 11,
        out_specs=pl.BlockSpec(memory_space=pltpu.VMEM),
        scratch_shapes=[
            pltpu.SMEM((1, micro), jnp.int32),
            pltpu.VMEM((micro, frames), jnp.int32),
            pltpu.VMEM((micro, frames), jnp.int32),
            pltpu.VMEM((taps, width), bf16),
            pltpu.VMEM((1, width), bf16),
            pltpu.VMEM((n, width), bf16),
            pltpu.VMEM((micro, frames, width), bf16),
            pltpu.VMEM((micro, frames, width), bf16),
            pltpu.VMEM((micro, slots, hidden), bf16),
            pltpu.VMEM((width, hidden), bf16),
            pltpu.VMEM((hidden, width), bf16),
            pltpu.VMEM((chunks, taps, LANES), f32),
            pltpu.VMEM((chunks, 1, LANES), f32),
            pltpu.VMEM((micro, *block), bf16),
            pltpu.VMEM((micro, *block), bf16),
            pltpu.VMEM((micro, *block), bf16),
            pltpu.VMEM((micro, *block), bf16),
            pltpu.VMEM((n, 1, LANES), f32),
            pltpu.VMEM((n, 1, LANES), f32),
            pltpu.VMEM((slots * chunks, LANES), f32),
            pltpu.VMEM((slots, width), bf16),
            pltpu.VMEM((chunks, frames + taps, LANES), f32),
            pltpu.VMEM((micro, chunks, frames, LANES), f32),
            pltpu.VMEM((micro, chunks, frames, LANES), f32),
            pltpu.VMEM((micro, frames, width), bf16),
            pltpu.VMEM((micro, slots, hidden), f32),
            pltpu.VMEM((micro, slots, hidden), f32),
            pltpu.VMEM((frames, width), f32),
            dma((2 * micro + 9,)),
            dma((micro,)),
            dma((micro,)),
            dma((micro,)),
            dma((micro,)),
            dma,
            dma,
        ],
        compiler_params=pltpu.CompilerParams(
            collective_id=0, has_side_effects=True, vmem_limit_bytes=32 * 1024 * 1024
        ),
        cost_estimate=pl.CostEstimate(
            flops=flops, bytes_accessed=8 * 1024 * 1024, transcendentals=0
        ),
    )(*operands)


def on_device(
    feat_saved,
    out_grad,
    lengths,
    expert_ids,
    slot_ids,
    expert_preact,
    conv_weight,
    norm_gain,
    centroids,
    w_in,
    w_out,
):
    section_count = lax.axis_size("section")
    micro_count = out_grad.shape[0]
    feats, routed, slots, preact = feat_saved[0], expert_ids[0], slot_ids[0], expert_preact[0]
    fixed = (conv_weight[0], norm_gain, centroids[0], w_in[0, 0], w_out[0, 0])
    if section_count == 1:
        return block_grads(out_grad, feats, lengths, routed, slots, preact, *fixed)[None]

    section_idx = lax.axis_index("section")
    route = [(i + 1, i) for i in range(section_count - 1)]

    def one_tick(tick_idx, carry):
        incoming, grads = carry
        micro_pos = tick_idx - (section_count - 1 - section_idx)
        is_valid = jnp.logical_and(micro_pos >= 0, micro_pos < micro_count)
        micro_sel = jnp.clip(micro_pos, 0, micro_count - 1)

        def pick(array):
            return lax.dynamic_slice_in_dim(array, micro_sel, 1, 0)

        grad_in = jnp.where(section_idx == section_count - 1, pick(out_grad), incoming)
        new_grad = block_grads(
            grad_in, pick(feats), pick(lengths), pick(routed), pick(slots), pick(preact), *fixed
        )
        updated = lax.dynamic_update_slice_in_dim(grads, new_grad, micro_sel, 0)
        grads = jnp.where(is_valid, updated, grads)
        return (lax.ppermute(new_grad, "section", route), grads)

    start = (jnp.zeros((1, *out_grad.shape[1:]), jnp.bfloat16), jnp.zeros_like(out_grad))
    _, grads = lax.fori_loop(0, section_count + micro_count - 1, one_tick, start)
    return grads[None]


def solution(mesh):
    in_specs = (
        P("section", None, "expert", None),
        P(None, "expert", None),
        P(None, "expert"),
        P("section", None, "expert"),
        P("section", None, "expert"),
        P("section", None, "expert", None),
        P("section", None, None),
        P("section", None),
        P("section", None, None),
        P("section", "expert", None, None),
        P("section", "expert", None, None),
    )
    out_specs = P("section", None, "expert", None)
    return jax.shard_map(
        on_device, mesh=mesh, in_specs=in_specs, out_specs=out_specs, check_vma=False
    )
```

```python
import functools
import math

import jax
import jax.numpy as jnp
from jax import lax
from jax.experimental import pallas as pl
from jax.experimental.pallas import tpu as pltpu
from jax.sharding import PartitionSpec as P

LANES = 128
SUB = 8
MESH = pl.DeviceIdType.MESH


def contract_last(left, right):
    return lax.dot_general(
        left, right, (((1,), (1,)), ((), ())), preferred_element_type=jnp.float32
    )


def to_column(row):
    size = row.shape[1]
    same = lax.broadcasted_iota(jnp.int32, (size, size), 0) == lax.broadcasted_iota(
        jnp.int32, (size, size), 1
    )
    wide = jnp.broadcast_to(row.astype(jnp.float32), (size, size))
    return jnp.sum(jnp.where(same, wide, 0.0), axis=1, keepdims=True).astype(jnp.int32)


def kernel(
    axis,
    n,
    slot_cap,
    length_hbm,
    routed_hbm,
    slot_hbm,
    conv_hbm,
    gain_hbm,
    cent_hbm,
    feat_hbm,
    grad_hbm,
    preact_hbm,
    w_in_hbm,
    w_out_hbm,
    out_ref,
    length_ref,
    routed_ref,
    slot_ref,
    conv_ref,
    gain_ref,
    cent_ref,
    feat_ref,
    grad_ref,
    preact_ref,
    w_in_ref,
    w_out_ref,
    taps_ref,
    gain_f,
    send_ref,
    recv_ref,
    back_ref,
    home_ref,
    gate_send,
    gate_recv,
    turn_ref,
    rows_ref,
    pad_ref,
    resid_ref,
    slope_ref,
    cent_rows,
    gelu_ref,
    gelu_slope_ref,
    slot_back,
    load_sem,
    send_sem,
    recv_sem,
    back_sem,
    home_sem,
    gate_send_sem,
    gate_recv_sem,
):
    micro, frames, width = feat_ref.shape
    stride = next(k for k in range(n // 3 + 1, 2 * n) if math.gcd(k, n) == 1)
    chunks = width // LANES
    slots = n * slot_cap
    tap_count = conv_ref.shape[0]
    low = tap_count // 2
    experts = n
    gate_span = LANES // micro
    me = lax.axis_index(axis)

    barrier = pltpu.get_barrier_semaphore()

    def greet(step, carry):
        pl.semaphore_signal(
            barrier, inc=1, device_id={axis: lax.rem(me + step, n)}, device_id_type=MESH
        )
        return carry

    def load(src, dst, at):
        return pltpu.make_async_copy(src, dst, load_sem.at[at])

    routed_load = load(routed_hbm, routed_ref, 2 * micro + 3)
    slot_load = load(slot_hbm, slot_ref, 2 * micro + 4)
    small_loads = [
        load(conv_hbm, conv_ref, 2 * micro + 5),
        load(gain_hbm, gain_ref, 2 * micro + 6),
        load(cent_hbm, cent_ref, 2 * micro + 7),
        load(length_hbm, length_ref, 2 * micro + 8),
    ]
    grad_loads = [load(grad_hbm.at[m], grad_ref.at[m], m) for m in range(micro)]
    feat_loads = [load(feat_hbm.at[m], feat_ref.at[m], micro + m) for m in range(micro)]
    pre_load = load(preact_hbm, preact_ref, 2 * micro)
    out_load = load(w_out_hbm, w_out_ref, 2 * micro + 1)
    in_load = load(w_in_hbm, w_in_ref, 2 * micro + 2)
    for copy in (routed_load, slot_load, *grad_loads):
        copy.start()
    lax.fori_loop(1, n, greet, 0)
    for copy in (*small_loads, *feat_loads, pre_load, out_load, in_load):
        copy.start()

    def cols(c):
        return pl.ds(c * LANES, LANES)

    def to_blocks(rows, dst):
        for c in range(chunks):
            turn_ref[pl.ds(c, slots, stride=chunks), :] = rows[:, c * LANES : (c + 1) * LANES]
        dst[...] = turn_ref[...].astype(jnp.bfloat16).reshape(dst.shape)

    def from_blocks(src):
        turn_ref[...] = src[...].reshape(turn_ref.shape).astype(jnp.float32)
        for c in range(chunks):
            rows_ref[:, cols(c)] = turn_ref[pl.ds(c, slots, stride=chunks), :].astype(jnp.bfloat16)

    def exchange(src, dst, sent, got):
        def post(step, carry):
            peer = lax.rem(me + step * stride, n)
            pltpu.make_async_remote_copy(
                src_ref=src.at[peer],
                dst_ref=dst.at[me],
                send_sem=sent,
                recv_sem=got,
                device_id={axis: peer},
                device_id_type=MESH,
            ).start()
            return carry

        lax.fori_loop(1, n, post, 0)
        pltpu.make_async_copy(src.at[me], dst.at[me], got).start()

    def arrived(dst, got):
        pltpu.make_async_copy(dst, dst, got).wait()

    def departed(src, sent):
        part = src.at[pl.ds(0, n - 1)]
        pltpu.make_async_copy(part, part, sent).wait()

    def dispatch(m):
        exchange(send_ref.at[m], recv_ref.at[m], send_sem.at[m], recv_sem.at[m])

    routed_load.wait()
    slot_load.wait()
    for m in range(micro):
        grad_loads[m].wait()
        target = routed_ref[m : m + 1, :] * slot_cap + slot_ref[m : m + 1, :]
        onehot = (lax.broadcasted_iota(jnp.int32, (slots, frames), 0) == target).astype(
            jnp.float32
        ).astype(jnp.bfloat16)
        bucket = jnp.dot(onehot, grad_ref[m], preferred_element_type=jnp.float32)
        to_blocks(bucket, send_ref.at[m])
        if m == 0:
            pl.semaphore_wait(barrier, n - 1)
            dispatch(m)

    for copy in small_loads:
        copy.wait()

    for c in range(chunks):
        taps_ref[c] = conv_ref[:, cols(c)].astype(jnp.float32)
        gain_f[c] = gain_ref[:, cols(c)].astype(jnp.float32)
        pad_ref[c, 0:low, :] = jnp.zeros((low, LANES), jnp.float32)
        pad_ref[c, low + frames :, :] = jnp.zeros((tap_count - low, LANES), jnp.float32)

    def conv(c, start, tap_of):
        acc = jnp.zeros((frames, LANES), jnp.float32)
        reach = (tap_count - 1) // SUB * SUB
        for offset in range(start, start + SUB):
            rows = pad_ref[c, offset : offset + frames + reach, :]
            for first in range(0, reach + 1, SUB):
                k = tap_of(offset + first)
                acc = acc + taps_ref[c, k : k + 1, :] * rows[first : first + frames, :]
        return acc

    frame_at = lax.broadcasted_iota(jnp.int32, (frames, 1), 0)

    masks, inv_all, gate_all, exp_all, slot_all, slot_hot = [], [], [], [], [], []
    def forward(m):
        feat_loads[m].wait()
        mask = (frame_at < length_ref[0, m]).astype(jnp.float32)
        routed = to_column(routed_ref[m : m + 1, :])
        slot_pos = to_column(slot_ref[m : m + 1, :])
        exp_hot = (
            lax.broadcasted_iota(jnp.int32, (frames, experts), 1) == routed
        ).astype(jnp.float32)
        cent_rows[m] = jnp.dot(
            exp_hot.astype(jnp.bfloat16), cent_ref[...], preferred_element_type=jnp.float32
        ).astype(jnp.bfloat16)

        def ahead(c, square):
            lanes = pl.ds(pl.multiple_of(c * LANES, LANES), LANES)
            feats = feat_ref[m, :, lanes].astype(jnp.float32)
            pad_ref[c, low : low + frames, :] = feats * mask
            acc = conv(c, 0, lambda first: first)
            sig = jax.nn.sigmoid(acc)
            resid = feats + mask * acc * sig
            resid_ref[m, c] = resid
            slope_ref[m, c] = mask * sig * (1.0 + acc * (1.0 - sig))
            return square + resid * resid

        square = lax.fori_loop(0, chunks, ahead, jnp.zeros((frames, LANES), jnp.float32))
        if m + 1 < micro:
            dispatch(m + 1)
        inv_rms = lax.rsqrt(jnp.sum(square, axis=1, keepdims=True) * (1.0 / width) + 1e-06)

        def scoring(c, total):
            lanes = pl.ds(pl.multiple_of(c * LANES, LANES), LANES)
            normed = (resid_ref[m, c] * inv_rms * gain_f[c]).astype(jnp.bfloat16)
            return total + normed.astype(jnp.float32) * cent_rows[m, :, lanes].astype(jnp.float32)

        score = lax.fori_loop(0, chunks, scoring, jnp.zeros((frames, LANES), jnp.float32))
        gate_all.append(jax.nn.sigmoid(jnp.sum(score, axis=1, keepdims=True)))
        masks.append(mask)
        inv_all.append(inv_rms)
        exp_all.append(exp_hot)
        slot_all.append(slot_pos)
        slot_hot.append(
            (
                lax.broadcasted_iota(jnp.int32, (frames, slots), 1)
                == routed * slot_cap + slot_pos
            ).astype(jnp.float32).astype(jnp.bfloat16)
        )

        if m == 0:
            pre_load.wait()
        act = preact_ref[m].astype(jnp.float32)
        cdf = 0.5 * (1.0 + lax.erf(act * (1.0 / math.sqrt(2.0))))
        gelu_ref[m] = act * cdf
        gelu_slope_ref[m] = cdf + act * jnp.exp(-0.5 * act * act) * (
            1.0 / math.sqrt(2.0 * math.pi)
        )

    slot_id = lax.broadcasted_iota(jnp.int32, (slots, LANES), 0)
    lane_id = lax.broadcasted_iota(jnp.int32, (slots, LANES), 1)
    group_first = lax.broadcasted_iota(jnp.int32, (n, slots), 0) * slot_cap
    group_slot = lax.broadcasted_iota(jnp.int32, (n, slots), 1)
    grouped = jnp.logical_and(
        group_slot >= group_first, group_slot < group_first + slot_cap
    ).astype(jnp.float32)
    def expert(m, gate_rows):
        if m == 0:
            out_load.wait()
            in_load.wait()
        arrived(recv_ref.at[m], recv_sem.at[m])
        from_blocks(recv_ref.at[m])
        hidden = contract_last(rows_ref[...], w_out_ref[...])
        gate = jnp.sum(hidden * gelu_ref[m], axis=1, keepdims=True)
        pre_grad = (hidden * gelu_slope_ref[m]).astype(jnp.bfloat16)
        spread = jnp.where(lax.rem(slot_id, slot_cap) + m * gate_span == lane_id, gate, 0.0)
        gate_rows = gate_rows + jnp.dot(
            grouped, spread, preferred_element_type=jnp.float32, precision=lax.Precision.HIGHEST
        )
        if m == micro - 1:
            gate_send[...] = gate_rows.reshape(gate_send.shape)
            exchange(gate_send, gate_recv, gate_send_sem, gate_recv_sem)
        to_blocks(contract_last(pre_grad, w_in_ref[...]), back_ref.at[m])
        exchange(back_ref.at[m], home_ref.at[m], back_sem.at[m], home_sem.at[m])
        return gate_rows

    gate_rows = jnp.zeros((n, LANES), jnp.float32)
    for m in range(micro):
        forward(m)
        gate_rows = expert(m, gate_rows)

    arrived(gate_recv, gate_recv_sem)
    frame_lane = lax.broadcasted_iota(jnp.int32, (frames, LANES), 1)
    for m in range(micro):
        mask, inv_rms, gate_val = masks[m], inv_all[m], gate_all[m]
        picked = jnp.dot(
            exp_all[m],
            gate_recv[...].reshape(n, LANES),
            preferred_element_type=jnp.float32,
            precision=lax.Precision.HIGHEST,
        )
        gate_grad = jnp.sum(
            jnp.where(frame_lane == slot_all[m] + m * gate_span, picked, 0.0),
            axis=1,
            keepdims=True,
        )
        cent_scale = gate_val * (1.0 - gate_val) * gate_grad
        arrived(home_ref.at[m], home_sem.at[m])
        from_blocks(home_ref.at[m])
        slot_back[...] = jnp.dot(slot_hot[m], rows_ref[...], preferred_element_type=jnp.float32)

        def scaling(c, total):
            lanes = pl.ds(pl.multiple_of(c * LANES, LANES), LANES)
            grad = gate_val * slot_back[:, lanes] + cent_scale * cent_rows[m, :, lanes].astype(
                jnp.float32
            )
            scaled = grad * gain_f[c]
            slot_back[:, lanes] = scaled
            return total + resid_ref[m, c] * scaled

        total = lax.fori_loop(0, chunks, scaling, jnp.zeros((frames, LANES), jnp.float32))
        mean = jnp.sum(total, axis=1, keepdims=True) * (1.0 / width)
        back_scale = inv_rms * inv_rms * inv_rms * mean

        def finish(c, carry):
            lanes = pl.ds(pl.multiple_of(c * LANES, LANES), LANES)
            resid_grad = (
                grad_ref[m, :, lanes].astype(jnp.float32)
                + inv_rms * slot_back[:, lanes]
                - resid_ref[m, c] * back_scale
            )
            pad_ref[c, low : low + frames, :] = slope_ref[m, c] * resid_grad
            acc = conv(c, 1, lambda first: 2 * low - first)
            out_ref[m, :, lanes] = (resid_grad + mask * acc).astype(jnp.bfloat16)
            return carry

        lax.fori_loop(0, chunks, finish, 0)

    for m in range(micro):
        departed(send_ref.at[m], send_sem.at[m])
        departed(back_ref.at[m], back_sem.at[m])
    departed(gate_send, gate_send_sem)


def block_grads(
    grads, feats, lengths, routed, slot_pos, preact, conv_k, gain, cent, weight_in, weight_out
):
    micro, frames, width = feats.shape
    n = lax.axis_size("expert")
    hidden = weight_in.shape[1]
    cap = preact.shape[1] // n
    whole_rows = 16 * LANES // math.gcd(16 * LANES, width)
    slot_cap = -(-cap // whole_rows) * whole_rows
    if slot_cap != cap:
        preact = jnp.pad(
            preact.reshape(micro, n, cap, hidden), ((0, 0), (0, 0), (0, slot_cap - cap), (0, 0))
        ).reshape(micro, n * slot_cap, hidden)
    slots = n * slot_cap
    chunks = width // LANES
    taps = conv_k.shape[0]
    block = (n, slot_cap * chunks, LANES)
    bf16, f32 = jnp.bfloat16, jnp.float32
    lengths = lengths.reshape(1, micro)
    held = (
        lengths, routed, slot_pos, conv_k, gain, cent, feats, grads, preact, weight_in, weight_out
    )
    operands = [pltpu.with_memory_space_constraint(x, pltpu.HBM) for x in held]
    in_hbm = pl.BlockSpec(memory_space=pltpu.HBM)
    dma = pltpu.SemaphoreType.DMA
    flops = micro * (4 * slots * width * hidden + 4 * frames * width * (taps + slots))
    return pl.pallas_call(
        functools.partial(kernel, "expert", n, slot_cap),
        out_shape=jax.ShapeDtypeStruct((micro, frames, width), bf16),
        in_specs=[in_hbm] * 11,
        out_specs=pl.BlockSpec(memory_space=pltpu.VMEM),
        scratch_shapes=[
            pltpu.SMEM((1, micro), jnp.int32),
            pltpu.VMEM((micro, frames), jnp.int32),
            pltpu.VMEM((micro, frames), jnp.int32),
            pltpu.VMEM((taps, width), bf16),
            pltpu.VMEM((1, width), bf16),
            pltpu.VMEM((n, width), bf16),
            pltpu.VMEM((micro, frames, width), bf16),
            pltpu.VMEM((micro, frames, width), bf16),
            pltpu.VMEM((micro, slots, hidden), bf16),
            pltpu.VMEM((width, hidden), bf16),
            pltpu.VMEM((hidden, width), bf16),
            pltpu.VMEM((chunks, taps, LANES), f32),
            pltpu.VMEM((chunks, 1, LANES), f32),
            pltpu.VMEM((micro, *block), bf16),
            pltpu.VMEM((micro, *block), bf16),
            pltpu.VMEM((micro, *block), bf16),
            pltpu.VMEM((micro, *block), bf16),
            pltpu.VMEM((n, 1, LANES), f32),
            pltpu.VMEM((n, 1, LANES), f32),
            pltpu.VMEM((slots * chunks, LANES), f32),
            pltpu.VMEM((slots, width), bf16),
            pltpu.VMEM((chunks, frames + taps, LANES), f32),
            pltpu.VMEM((micro, chunks, frames, LANES), f32),
            pltpu.VMEM((micro, chunks, frames, LANES), f32),
            pltpu.VMEM((micro, frames, width), bf16),
            pltpu.VMEM((micro, slots, hidden), f32),
            pltpu.VMEM((micro, slots, hidden), f32),
            pltpu.VMEM((frames, width), f32),
            dma((2 * micro + 9,)),
            dma((micro,)),
            dma((micro,)),
            dma((micro,)),
            dma((micro,)),
            dma,
            dma,
        ],
        compiler_params=pltpu.CompilerParams(
            collective_id=0, has_side_effects=True, vmem_limit_bytes=32 * 1024 * 1024
        ),
        cost_estimate=pl.CostEstimate(
            flops=flops, bytes_accessed=8 * 1024 * 1024, transcendentals=0
        ),
    )(*operands)


def on_device(
    feat_saved,
    out_grad,
    lengths,
    expert_ids,
    slot_ids,
    expert_preact,
    conv_weight,
    norm_gain,
    centroids,
    w_in,
    w_out,
):
    section_count = lax.axis_size("section")
    micro_count = out_grad.shape[0]
    feats, routed, slots, preact = feat_saved[0], expert_ids[0], slot_ids[0], expert_preact[0]
    fixed = (conv_weight[0], norm_gain, centroids[0], w_in[0, 0], w_out[0, 0])
    if section_count == 1:
        return block_grads(out_grad, feats, lengths, routed, slots, preact, *fixed)[None]

    section_idx = lax.axis_index("section")
    route = [(i + 1, i) for i in range(section_count - 1)]

    def one_tick(tick_idx, carry):
        incoming, grads = carry
        micro_pos = tick_idx - (section_count - 1 - section_idx)
        is_valid = jnp.logical_and(micro_pos >= 0, micro_pos < micro_count)
        micro_sel = jnp.clip(micro_pos, 0, micro_count - 1)

        def pick(array):
            return lax.dynamic_slice_in_dim(array, micro_sel, 1, 0)

        grad_in = jnp.where(section_idx == section_count - 1, pick(out_grad), incoming)
        new_grad = block_grads(
            grad_in, pick(feats), pick(lengths), pick(routed), pick(slots), pick(preact), *fixed
        )
        updated = lax.dynamic_update_slice_in_dim(grads, new_grad, micro_sel, 0)
        grads = jnp.where(is_valid, updated, grads)
        return (lax.ppermute(new_grad, "section", route), grads)

    start = (jnp.zeros((1, *out_grad.shape[1:]), jnp.bfloat16), jnp.zeros_like(out_grad))
    _, grads = lax.fori_loop(0, section_count + micro_count - 1, one_tick, start)
    return grads[None]


def solution(mesh):
    in_specs = (
        P("section", None, "expert", None),
        P(None, "expert", None),
        P(None, "expert"),
        P("section", None, "expert"),
        P("section", None, "expert"),
        P("section", None, "expert", None),
        P("section", None, None),
        P("section", None),
        P("section", None, None),
        P("section", "expert", None, None),
        P("section", "expert", None, None),
    )
    out_specs = P("section", None, "expert", None)
    return jax.shard_map(
        on_device, mesh=mesh, in_specs=in_specs, out_specs=out_specs, check_vma=False
    )
```

```python
import functools
import math

import jax
import jax.numpy as jnp
from jax import lax
from jax.experimental import pallas as pl
from jax.experimental.pallas import tpu as pltpu
from jax.sharding import PartitionSpec as P

LANES = 128
SUB = 8
MESH = pl.DeviceIdType.MESH


def contract_last(left, right):
    return lax.dot_general(
        left, right, (((1,), (1,)), ((), ())), preferred_element_type=jnp.float32
    )


def to_column(row):
    size = row.shape[1]
    same = lax.broadcasted_iota(jnp.int32, (size, size), 0) == lax.broadcasted_iota(
        jnp.int32, (size, size), 1
    )
    wide = jnp.broadcast_to(row.astype(jnp.float32), (size, size))
    return jnp.sum(jnp.where(same, wide, 0.0), axis=1, keepdims=True).astype(jnp.int32)


def kernel(
    axis,
    n,
    slot_cap,
    length_hbm,
    routed_hbm,
    slot_hbm,
    conv_hbm,
    gain_hbm,
    cent_hbm,
    feat_hbm,
    grad_hbm,
    preact_hbm,
    w_in_hbm,
    w_out_hbm,
    out_ref,
    length_ref,
    routed_ref,
    slot_ref,
    conv_ref,
    gain_ref,
    cent_ref,
    feat_ref,
    grad_ref,
    preact_ref,
    w_in_ref,
    w_out_ref,
    taps_ref,
    gain_f,
    send_ref,
    recv_ref,
    back_ref,
    home_ref,
    gate_send,
    gate_recv,
    turn_ref,
    rows_ref,
    pad_ref,
    resid_ref,
    slope_ref,
    cent_rows,
    gelu_ref,
    gelu_slope_ref,
    slot_back,
    load_sem,
    send_sem,
    recv_sem,
    back_sem,
    home_sem,
    gate_send_sem,
    gate_recv_sem,
):
    micro, frames, width = feat_ref.shape
    stride = next(k for k in range(n // 3 + 1, 2 * n) if math.gcd(k, n) == 1)
    chunks = width // LANES
    slots = n * slot_cap
    tap_count = conv_ref.shape[0]
    low = tap_count // 2
    experts = n
    gate_span = LANES // micro
    me = lax.axis_index(axis)

    barrier = pltpu.get_barrier_semaphore()

    def greet(step, carry):
        pl.semaphore_signal(
            barrier, inc=1, device_id={axis: lax.rem(me + step, n)}, device_id_type=MESH
        )
        return carry

    def load(src, dst, at):
        return pltpu.make_async_copy(src, dst, load_sem.at[at])

    routed_load = load(routed_hbm, routed_ref, 2 * micro + 3)
    slot_load = load(slot_hbm, slot_ref, 2 * micro + 4)
    small_loads = [
        load(conv_hbm, conv_ref, 2 * micro + 5),
        load(gain_hbm, gain_ref, 2 * micro + 6),
        load(cent_hbm, cent_ref, 2 * micro + 7),
        load(length_hbm, length_ref, 2 * micro + 8),
    ]
    grad_loads = [load(grad_hbm.at[m], grad_ref.at[m], m) for m in range(micro)]
    feat_loads = [load(feat_hbm.at[m], feat_ref.at[m], micro + m) for m in range(micro)]
    pre_load = load(preact_hbm, preact_ref, 2 * micro)
    out_load = load(w_out_hbm, w_out_ref, 2 * micro + 1)
    in_load = load(w_in_hbm, w_in_ref, 2 * micro + 2)
    for copy in (routed_load, slot_load, *grad_loads):
        copy.start()
    lax.fori_loop(1, n, greet, 0)
    for copy in (*small_loads, *feat_loads, pre_load, out_load, in_load):
        copy.start()

    def cols(c):
        return pl.ds(c * LANES, LANES)

    def to_blocks(rows, dst):
        for c in range(chunks):
            turn_ref[pl.ds(c, slots, stride=chunks), :] = rows[:, c * LANES : (c + 1) * LANES]
        dst[...] = turn_ref[...].astype(jnp.bfloat16).reshape(dst.shape)

    def from_blocks(src):
        turn_ref[...] = src[...].reshape(turn_ref.shape).astype(jnp.float32)
        for c in range(chunks):
            rows_ref[:, cols(c)] = turn_ref[pl.ds(c, slots, stride=chunks), :].astype(jnp.bfloat16)

    def exchange(src, dst, sent, got, beside=False):
        def post(step, carry):
            peer = lax.rem(me + step * stride, n)
            pltpu.make_async_remote_copy(
                src_ref=src.at[peer],
                dst_ref=dst.at[me],
                send_sem=sent,
                recv_sem=got,
                device_id={axis: peer},
                device_id_type=MESH,
            ).start()
            return carry

        pltpu.make_async_copy(src.at[me], dst.at[me], got).start()
        if beside:
            return post
        lax.fori_loop(1, n, post, 0)
        return None

    def arrived(dst, got):
        pltpu.make_async_copy(dst, dst, got).wait()

    def departed(src, sent):
        part = src.at[pl.ds(0, n - 1)]
        pltpu.make_async_copy(part, part, sent).wait()

    def dispatch(m, beside=False):
        return exchange(
            send_ref.at[m], recv_ref.at[m], send_sem.at[m], recv_sem.at[m], beside
        )

    routed_load.wait()
    slot_load.wait()
    for m in range(micro):
        grad_loads[m].wait()
        target = routed_ref[m : m + 1, :] * slot_cap + slot_ref[m : m + 1, :]
        onehot = (lax.broadcasted_iota(jnp.int32, (slots, frames), 0) == target).astype(
            jnp.float32
        ).astype(jnp.bfloat16)
        bucket = jnp.dot(onehot, grad_ref[m], preferred_element_type=jnp.float32)
        to_blocks(bucket, send_ref.at[m])
        if m == 0:
            pl.semaphore_wait(barrier, n - 1)
            dispatch(m)

    for copy in small_loads:
        copy.wait()

    for c in range(chunks):
        taps_ref[c] = conv_ref[:, cols(c)].astype(jnp.float32)
        gain_f[c] = gain_ref[:, cols(c)].astype(jnp.float32)
        pad_ref[c, 0:low, :] = jnp.zeros((low, LANES), jnp.float32)
        pad_ref[c, low + frames :, :] = jnp.zeros((tap_count - low, LANES), jnp.float32)

    def conv(c, start, tap_of):
        acc = jnp.zeros((frames, LANES), jnp.float32)
        reach = (tap_count - 1) // SUB * SUB
        for offset in range(start, start + SUB):
            rows = pad_ref[c, offset : offset + frames + reach, :]
            for first in range(0, reach + 1, SUB):
                k = tap_of(offset + first)
                acc = acc + taps_ref[c, k : k + 1, :] * rows[first : first + frames, :]
        return acc

    frame_at = lax.broadcasted_iota(jnp.int32, (frames, 1), 0)

    masks, inv_all, gate_all, exp_all, slot_all, slot_hot = [], [], [], [], [], []
    def forward(m, posts):
        feat_loads[m].wait()
        mask = (frame_at < length_ref[0, m]).astype(jnp.float32)
        routed = to_column(routed_ref[m : m + 1, :])
        slot_pos = to_column(slot_ref[m : m + 1, :])
        exp_hot = (
            lax.broadcasted_iota(jnp.int32, (frames, experts), 1) == routed
        ).astype(jnp.float32)
        cent_rows[m] = jnp.dot(
            exp_hot.astype(jnp.bfloat16), cent_ref[...], preferred_element_type=jnp.float32
        ).astype(jnp.bfloat16)

        share = (n - 1) // chunks

        def ahead(c, square):
            for post in posts:
                for j in range(share):
                    post(1 + c * share + j, 0)
            lanes = pl.ds(pl.multiple_of(c * LANES, LANES), LANES)
            feats = feat_ref[m, :, lanes].astype(jnp.float32)
            pad_ref[c, low : low + frames, :] = feats * mask
            acc = conv(c, 0, lambda first: first)
            sig = jax.nn.sigmoid(acc)
            resid = feats + mask * acc * sig
            resid_ref[m, c] = resid
            slope_ref[m, c] = mask * sig * (1.0 + acc * (1.0 - sig))
            return square + resid * resid

        square = lax.fori_loop(0, chunks, ahead, jnp.zeros((frames, LANES), jnp.float32))
        for post in posts:
            lax.fori_loop(1 + chunks * share, n, post, 0)
        inv_rms = lax.rsqrt(jnp.sum(square, axis=1, keepdims=True) * (1.0 / width) + 1e-06)

        def scoring(c, total):
            lanes = pl.ds(pl.multiple_of(c * LANES, LANES), LANES)
            normed = (resid_ref[m, c] * inv_rms * gain_f[c]).astype(jnp.bfloat16)
            return total + normed.astype(jnp.float32) * cent_rows[m, :, lanes].astype(jnp.float32)

        score = lax.fori_loop(0, chunks, scoring, jnp.zeros((frames, LANES), jnp.float32))
        gate_all.append(jax.nn.sigmoid(jnp.sum(score, axis=1, keepdims=True)))
        masks.append(mask)
        inv_all.append(inv_rms)
        exp_all.append(exp_hot)
        slot_all.append(slot_pos)
        slot_hot.append(
            (
                lax.broadcasted_iota(jnp.int32, (frames, slots), 1)
                == routed * slot_cap + slot_pos
            ).astype(jnp.float32).astype(jnp.bfloat16)
        )

        if m == 0:
            pre_load.wait()
        act = preact_ref[m].astype(jnp.float32)
        cdf = 0.5 * (1.0 + lax.erf(act * (1.0 / math.sqrt(2.0))))
        gelu_ref[m] = act * cdf
        gelu_slope_ref[m] = cdf + act * jnp.exp(-0.5 * act * act) * (
            1.0 / math.sqrt(2.0 * math.pi)
        )

    slot_id = lax.broadcasted_iota(jnp.int32, (slots, LANES), 0)
    lane_id = lax.broadcasted_iota(jnp.int32, (slots, LANES), 1)
    group_first = lax.broadcasted_iota(jnp.int32, (n, slots), 0) * slot_cap
    group_slot = lax.broadcasted_iota(jnp.int32, (n, slots), 1)
    grouped = jnp.logical_and(
        group_slot >= group_first, group_slot < group_first + slot_cap
    ).astype(jnp.float32)
    def expert(m, gate_rows):
        if m == 0:
            out_load.wait()
            in_load.wait()
        arrived(recv_ref.at[m], recv_sem.at[m])
        from_blocks(recv_ref.at[m])
        hidden = contract_last(rows_ref[...], w_out_ref[...])
        gate = jnp.sum(hidden * gelu_ref[m], axis=1, keepdims=True)
        pre_grad = (hidden * gelu_slope_ref[m]).astype(jnp.bfloat16)
        spread = jnp.where(lax.rem(slot_id, slot_cap) + m * gate_span == lane_id, gate, 0.0)
        gate_rows = gate_rows + jnp.dot(
            grouped, spread, preferred_element_type=jnp.float32, precision=lax.Precision.HIGHEST
        )
        if m == micro - 1:
            gate_send[...] = gate_rows.reshape(gate_send.shape)
            exchange(gate_send, gate_recv, gate_send_sem, gate_recv_sem)
        to_blocks(contract_last(pre_grad, w_in_ref[...]), back_ref.at[m])
        post = exchange(
            back_ref.at[m], home_ref.at[m], back_sem.at[m], home_sem.at[m], m + 1 < micro
        )
        return gate_rows, post

    gate_rows = jnp.zeros((n, LANES), jnp.float32)
    for m in range(micro):
        posts = [back_post] if m > 0 else []
        if m + 1 < micro:
            posts.append(dispatch(m + 1, True))
        forward(m, posts)
        gate_rows, back_post = expert(m, gate_rows)

    arrived(gate_recv, gate_recv_sem)
    frame_lane = lax.broadcasted_iota(jnp.int32, (frames, LANES), 1)
    for m in range(micro):
        mask, inv_rms, gate_val = masks[m], inv_all[m], gate_all[m]
        picked = jnp.dot(
            exp_all[m],
            gate_recv[...].reshape(n, LANES),
            preferred_element_type=jnp.float32,
            precision=lax.Precision.HIGHEST,
        )
        gate_grad = jnp.sum(
            jnp.where(frame_lane == slot_all[m] + m * gate_span, picked, 0.0),
            axis=1,
            keepdims=True,
        )
        cent_scale = gate_val * (1.0 - gate_val) * gate_grad
        arrived(home_ref.at[m], home_sem.at[m])
        from_blocks(home_ref.at[m])
        slot_back[...] = jnp.dot(slot_hot[m], rows_ref[...], preferred_element_type=jnp.float32)

        def scaling(c, total):
            lanes = pl.ds(pl.multiple_of(c * LANES, LANES), LANES)
            grad = gate_val * slot_back[:, lanes] + cent_scale * cent_rows[m, :, lanes].astype(
                jnp.float32
            )
            scaled = grad * gain_f[c]
            slot_back[:, lanes] = scaled
            return total + resid_ref[m, c] * scaled

        total = lax.fori_loop(0, chunks, scaling, jnp.zeros((frames, LANES), jnp.float32))
        mean = jnp.sum(total, axis=1, keepdims=True) * (1.0 / width)
        back_scale = inv_rms * inv_rms * inv_rms * mean

        def finish(c, carry):
            lanes = pl.ds(pl.multiple_of(c * LANES, LANES), LANES)
            resid_grad = (
                grad_ref[m, :, lanes].astype(jnp.float32)
                + inv_rms * slot_back[:, lanes]
                - resid_ref[m, c] * back_scale
            )
            pad_ref[c, low : low + frames, :] = slope_ref[m, c] * resid_grad
            acc = conv(c, 1, lambda first: 2 * low - first)
            out_ref[m, :, lanes] = (resid_grad + mask * acc).astype(jnp.bfloat16)
            return carry

        lax.fori_loop(0, chunks, finish, 0)

    for m in range(micro):
        departed(send_ref.at[m], send_sem.at[m])
        departed(back_ref.at[m], back_sem.at[m])
    departed(gate_send, gate_send_sem)


def block_grads(
    grads, feats, lengths, routed, slot_pos, preact, conv_k, gain, cent, weight_in, weight_out
):
    micro, frames, width = feats.shape
    n = lax.axis_size("expert")
    hidden = weight_in.shape[1]
    cap = preact.shape[1] // n
    whole_rows = 16 * LANES // math.gcd(16 * LANES, width)
    slot_cap = -(-cap // whole_rows) * whole_rows
    if slot_cap != cap:
        preact = jnp.pad(
            preact.reshape(micro, n, cap, hidden), ((0, 0), (0, 0), (0, slot_cap - cap), (0, 0))
        ).reshape(micro, n * slot_cap, hidden)
    slots = n * slot_cap
    chunks = width // LANES
    taps = conv_k.shape[0]
    block = (n, slot_cap * chunks, LANES)
    bf16, f32 = jnp.bfloat16, jnp.float32
    lengths = lengths.reshape(1, micro)
    held = (
        lengths, routed, slot_pos, conv_k, gain, cent, feats, grads, preact, weight_in, weight_out
    )
    operands = [pltpu.with_memory_space_constraint(x, pltpu.HBM) for x in held]
    in_hbm = pl.BlockSpec(memory_space=pltpu.HBM)
    dma = pltpu.SemaphoreType.DMA
    flops = micro * (4 * slots * width * hidden + 4 * frames * width * (taps + slots))
    return pl.pallas_call(
        functools.partial(kernel, "expert", n, slot_cap),
        out_shape=jax.ShapeDtypeStruct((micro, frames, width), bf16),
        in_specs=[in_hbm] * 11,
        out_specs=pl.BlockSpec(memory_space=pltpu.VMEM),
        scratch_shapes=[
            pltpu.SMEM((1, micro), jnp.int32),
            pltpu.VMEM((micro, frames), jnp.int32),
            pltpu.VMEM((micro, frames), jnp.int32),
            pltpu.VMEM((taps, width), bf16),
            pltpu.VMEM((1, width), bf16),
            pltpu.VMEM((n, width), bf16),
            pltpu.VMEM((micro, frames, width), bf16),
            pltpu.VMEM((micro, frames, width), bf16),
            pltpu.VMEM((micro, slots, hidden), bf16),
            pltpu.VMEM((width, hidden), bf16),
            pltpu.VMEM((hidden, width), bf16),
            pltpu.VMEM((chunks, taps, LANES), f32),
            pltpu.VMEM((chunks, 1, LANES), f32),
            pltpu.VMEM((micro, *block), bf16),
            pltpu.VMEM((micro, *block), bf16),
            pltpu.VMEM((micro, *block), bf16),
            pltpu.VMEM((micro, *block), bf16),
            pltpu.VMEM((n, 1, LANES), f32),
            pltpu.VMEM((n, 1, LANES), f32),
            pltpu.VMEM((slots * chunks, LANES), f32),
            pltpu.VMEM((slots, width), bf16),
            pltpu.VMEM((chunks, frames + taps, LANES), f32),
            pltpu.VMEM((micro, chunks, frames, LANES), f32),
            pltpu.VMEM((micro, chunks, frames, LANES), f32),
            pltpu.VMEM((micro, frames, width), bf16),
            pltpu.VMEM((micro, slots, hidden), f32),
            pltpu.VMEM((micro, slots, hidden), f32),
            pltpu.VMEM((frames, width), f32),
            dma((2 * micro + 9,)),
            dma((micro,)),
            dma((micro,)),
            dma((micro,)),
            dma((micro,)),
            dma,
            dma,
        ],
        compiler_params=pltpu.CompilerParams(
            collective_id=0, has_side_effects=True, vmem_limit_bytes=32 * 1024 * 1024
        ),
        cost_estimate=pl.CostEstimate(
            flops=flops, bytes_accessed=8 * 1024 * 1024, transcendentals=0
        ),
    )(*operands)


def on_device(
    feat_saved,
    out_grad,
    lengths,
    expert_ids,
    slot_ids,
    expert_preact,
    conv_weight,
    norm_gain,
    centroids,
    w_in,
    w_out,
):
    section_count = lax.axis_size("section")
    micro_count = out_grad.shape[0]
    feats, routed, slots, preact = feat_saved[0], expert_ids[0], slot_ids[0], expert_preact[0]
    fixed = (conv_weight[0], norm_gain, centroids[0], w_in[0, 0], w_out[0, 0])
    if section_count == 1:
        return block_grads(out_grad, feats, lengths, routed, slots, preact, *fixed)[None]

    section_idx = lax.axis_index("section")
    route = [(i + 1, i) for i in range(section_count - 1)]

    def one_tick(tick_idx, carry):
        incoming, grads = carry
        micro_pos = tick_idx - (section_count - 1 - section_idx)
        is_valid = jnp.logical_and(micro_pos >= 0, micro_pos < micro_count)
        micro_sel = jnp.clip(micro_pos, 0, micro_count - 1)

        def pick(array):
            return lax.dynamic_slice_in_dim(array, micro_sel, 1, 0)

        grad_in = jnp.where(section_idx == section_count - 1, pick(out_grad), incoming)
        new_grad = block_grads(
            grad_in, pick(feats), pick(lengths), pick(routed), pick(slots), pick(preact), *fixed
        )
        updated = lax.dynamic_update_slice_in_dim(grads, new_grad, micro_sel, 0)
        grads = jnp.where(is_valid, updated, grads)
        return (lax.ppermute(new_grad, "section", route), grads)

    start = (jnp.zeros((1, *out_grad.shape[1:]), jnp.bfloat16), jnp.zeros_like(out_grad))
    _, grads = lax.fori_loop(0, section_count + micro_count - 1, one_tick, start)
    return grads[None]


def solution(mesh):
    in_specs = (
        P("section", None, "expert", None),
        P(None, "expert", None),
        P(None, "expert"),
        P("section", None, "expert"),
        P("section", None, "expert"),
        P("section", None, "expert", None),
        P("section", None, None),
        P("section", None),
        P("section", None, None),
        P("section", "expert", None, None),
        P("section", "expert", None, None),
    )
    out_specs = P("section", None, "expert", None)
    return jax.shard_map(
        on_device, mesh=mesh, in_specs=in_specs, out_specs=out_specs, check_vma=False
    )
```

```python
import functools
import math

import jax
import jax.numpy as jnp
from jax import lax
from jax.experimental import pallas as pl
from jax.experimental.pallas import tpu as pltpu
from jax.sharding import PartitionSpec as P

LANES = 128
SUB = 8
MESH = pl.DeviceIdType.MESH


def contract_last(left, right):
    return lax.dot_general(
        left, right, (((1,), (1,)), ((), ())), preferred_element_type=jnp.float32
    )


def to_column(row):
    size = row.shape[1]
    same = lax.broadcasted_iota(jnp.int32, (size, size), 0) == lax.broadcasted_iota(
        jnp.int32, (size, size), 1
    )
    wide = jnp.broadcast_to(row.astype(jnp.float32), (size, size))
    return jnp.sum(jnp.where(same, wide, 0.0), axis=1, keepdims=True).astype(jnp.int32)


def kernel(
    axis,
    n,
    slot_cap,
    length_hbm,
    routed_hbm,
    slot_hbm,
    conv_hbm,
    gain_hbm,
    cent_hbm,
    feat_hbm,
    grad_hbm,
    preact_hbm,
    w_in_hbm,
    w_out_hbm,
    out_ref,
    length_ref,
    routed_ref,
    slot_ref,
    conv_ref,
    gain_ref,
    cent_ref,
    feat_ref,
    grad_ref,
    preact_ref,
    w_in_ref,
    w_out_ref,
    taps_ref,
    gain_f,
    send_ref,
    recv_ref,
    back_ref,
    home_ref,
    gate_send,
    gate_recv,
    turn_ref,
    rows_ref,
    pad_ref,
    resid_ref,
    slope_ref,
    cent_rows,
    gelu_ref,
    gelu_slope_ref,
    slot_back,
    load_sem,
    send_sem,
    recv_sem,
    back_sem,
    home_sem,
    gate_send_sem,
    gate_recv_sem,
):
    micro, frames, width = feat_ref.shape
    chunks = width // LANES
    slots = n * slot_cap
    tap_count = conv_ref.shape[0]
    low = tap_count // 2
    experts = n
    gate_span = LANES // micro
    me = lax.axis_index(axis)

    barrier = pltpu.get_barrier_semaphore()

    def greet(step, carry):
        pl.semaphore_signal(
            barrier, inc=1, device_id={axis: lax.rem(me + step, n)}, device_id_type=MESH
        )
        return carry

    def load(src, dst, at):
        return pltpu.make_async_copy(src, dst, load_sem.at[at])

    routed_load = load(routed_hbm, routed_ref, 2 * micro + 3)
    slot_load = load(slot_hbm, slot_ref, 2 * micro + 4)
    small_loads = [
        load(conv_hbm, conv_ref, 2 * micro + 5),
        load(gain_hbm, gain_ref, 2 * micro + 6),
        load(cent_hbm, cent_ref, 2 * micro + 7),
        load(length_hbm, length_ref, 2 * micro + 8),
    ]
    grad_loads = [load(grad_hbm.at[m], grad_ref.at[m], m) for m in range(micro)]
    feat_loads = [load(feat_hbm.at[m], feat_ref.at[m], micro + m) for m in range(micro)]
    pre_load = load(preact_hbm, preact_ref, 2 * micro)
    out_load = load(w_out_hbm, w_out_ref, 2 * micro + 1)
    in_load = load(w_in_hbm, w_in_ref, 2 * micro + 2)
    for copy in (routed_load, slot_load, *grad_loads):
        copy.start()
    lax.fori_loop(1, n, greet, 0)
    for copy in (*small_loads, *feat_loads, pre_load, out_load, in_load):
        copy.start()

    def cols(c):
        return pl.ds(c * LANES, LANES)

    def to_blocks(rows, dst):
        for c in range(chunks):
            turn_ref[pl.ds(c, slots, stride=chunks), :] = rows[:, c * LANES : (c + 1) * LANES]
        dst[...] = turn_ref[...].astype(jnp.bfloat16).reshape(dst.shape)

    def from_blocks(src):
        turn_ref[...] = src[...].reshape(turn_ref.shape).astype(jnp.float32)
        for c in range(chunks):
            rows_ref[:, cols(c)] = turn_ref[pl.ds(c, slots, stride=chunks), :].astype(jnp.bfloat16)

    def exchange(src, dst, sent, got):
        def post(step, carry):
            side = 2 * lax.rem(step + 1, 2) - 1
            peer = lax.rem(me + n // 2 + side * lax.div(step, 2), n)
            pltpu.make_async_remote_copy(
                src_ref=src.at[peer],
                dst_ref=dst.at[me],
                send_sem=sent,
                recv_sem=got,
                device_id={axis: peer},
                device_id_type=MESH,
            ).start()
            return carry

        lax.fori_loop(1, n, post, 0)
        pltpu.make_async_copy(src.at[me], dst.at[me], got).start()

    def arrived(dst, got):
        pltpu.make_async_copy(dst, dst, got).wait()

    def departed(src, sent):
        part = src.at[pl.ds(0, n - 1)]
        pltpu.make_async_copy(part, part, sent).wait()

    def dispatch(m):
        exchange(send_ref.at[m], recv_ref.at[m], send_sem.at[m], recv_sem.at[m])

    routed_load.wait()
    slot_load.wait()
    for m in range(micro):
        grad_loads[m].wait()
        target = routed_ref[m : m + 1, :] * slot_cap + slot_ref[m : m + 1, :]
        onehot = (lax.broadcasted_iota(jnp.int32, (slots, frames), 0) == target).astype(
            jnp.float32
        ).astype(jnp.bfloat16)
        bucket = jnp.dot(onehot, grad_ref[m], preferred_element_type=jnp.float32)
        to_blocks(bucket, send_ref.at[m])
        if m == 0:
            pl.semaphore_wait(barrier, n - 1)
            dispatch(m)

    for copy in small_loads:
        copy.wait()

    for c in range(chunks):
        taps_ref[c] = conv_ref[:, cols(c)].astype(jnp.float32)
        gain_f[c] = gain_ref[:, cols(c)].astype(jnp.float32)
        pad_ref[c, 0:low, :] = jnp.zeros((low, LANES), jnp.float32)
        pad_ref[c, low + frames :, :] = jnp.zeros((tap_count - low, LANES), jnp.float32)

    def conv(c, start, tap_of):
        acc = jnp.zeros((frames, LANES), jnp.float32)
        reach = (tap_count - 1) // SUB * SUB
        for offset in range(start, start + SUB):
            rows = pad_ref[c, offset : offset + frames + reach, :]
            for first in range(0, reach + 1, SUB):
                k = tap_of(offset + first)
                acc = acc + taps_ref[c, k : k + 1, :] * rows[first : first + frames, :]
        return acc

    frame_at = lax.broadcasted_iota(jnp.int32, (frames, 1), 0)

    masks, inv_all, gate_all, exp_all, slot_all, slot_hot = [], [], [], [], [], []
    for m in range(micro):
        feat_loads[m].wait()
        mask = (frame_at < length_ref[0, m]).astype(jnp.float32)
        routed = to_column(routed_ref[m : m + 1, :])
        slot_pos = to_column(slot_ref[m : m + 1, :])
        exp_hot = (
            lax.broadcasted_iota(jnp.int32, (frames, experts), 1) == routed
        ).astype(jnp.float32)
        cent_rows[m] = jnp.dot(
            exp_hot.astype(jnp.bfloat16), cent_ref[...], preferred_element_type=jnp.float32
        ).astype(jnp.bfloat16)

        def ahead(c, square):
            lanes = pl.ds(pl.multiple_of(c * LANES, LANES), LANES)
            feats = feat_ref[m, :, lanes].astype(jnp.float32)
            pad_ref[c, low : low + frames, :] = feats * mask
            acc = conv(c, 0, lambda first: first)
            sig = jax.nn.sigmoid(acc)
            resid = feats + mask * acc * sig
            resid_ref[m, c] = resid
            slope_ref[m, c] = mask * sig * (1.0 + acc * (1.0 - sig))
            return square + resid * resid

        square = lax.fori_loop(0, chunks, ahead, jnp.zeros((frames, LANES), jnp.float32))
        if m + 1 < micro:
            dispatch(m + 1)
        inv_rms = lax.rsqrt(jnp.sum(square, axis=1, keepdims=True) * (1.0 / width) + 1e-06)

        def scoring(c, total):
            lanes = pl.ds(pl.multiple_of(c * LANES, LANES), LANES)
            normed = (resid_ref[m, c] * inv_rms * gain_f[c]).astype(jnp.bfloat16)
            return total + normed.astype(jnp.float32) * cent_rows[m, :, lanes].astype(jnp.float32)

        score = lax.fori_loop(0, chunks, scoring, jnp.zeros((frames, LANES), jnp.float32))
        gate_all.append(jax.nn.sigmoid(jnp.sum(score, axis=1, keepdims=True)))
        masks.append(mask)
        inv_all.append(inv_rms)
        exp_all.append(exp_hot)
        slot_all.append(slot_pos)
        slot_hot.append(
            (
                lax.broadcasted_iota(jnp.int32, (frames, slots), 1)
                == routed * slot_cap + slot_pos
            ).astype(jnp.float32).astype(jnp.bfloat16)
        )

        if m == 0:
            pre_load.wait()
        act = preact_ref[m].astype(jnp.float32)
        cdf = 0.5 * (1.0 + lax.erf(act * (1.0 / math.sqrt(2.0))))
        gelu_ref[m] = act * cdf
        gelu_slope_ref[m] = cdf + act * jnp.exp(-0.5 * act * act) * (
            1.0 / math.sqrt(2.0 * math.pi)
        )

    out_load.wait()
    in_load.wait()
    gate_rows = jnp.zeros((n, LANES), jnp.float32)
    slot_id = lax.broadcasted_iota(jnp.int32, (slots, LANES), 0)
    lane_id = lax.broadcasted_iota(jnp.int32, (slots, LANES), 1)
    group_first = lax.broadcasted_iota(jnp.int32, (n, slots), 0) * slot_cap
    group_slot = lax.broadcasted_iota(jnp.int32, (n, slots), 1)
    grouped = jnp.logical_and(
        group_slot >= group_first, group_slot < group_first + slot_cap
    ).astype(jnp.float32)
    for m in range(micro):
        arrived(recv_ref.at[m], recv_sem.at[m])
        from_blocks(recv_ref.at[m])
        hidden = contract_last(rows_ref[...], w_out_ref[...])
        gate = jnp.sum(hidden * gelu_ref[m], axis=1, keepdims=True)
        pre_grad = (hidden * gelu_slope_ref[m]).astype(jnp.bfloat16)
        spread = jnp.where(lax.rem(slot_id, slot_cap) + m * gate_span == lane_id, gate, 0.0)
        gate_rows = gate_rows + jnp.dot(
            grouped, spread, preferred_element_type=jnp.float32, precision=lax.Precision.HIGHEST
        )
        if m == micro - 1:
            gate_send[...] = gate_rows.reshape(gate_send.shape)
            exchange(gate_send, gate_recv, gate_send_sem, gate_recv_sem)
        to_blocks(contract_last(pre_grad, w_in_ref[...]), back_ref.at[m])
        exchange(back_ref.at[m], home_ref.at[m], back_sem.at[m], home_sem.at[m])

    arrived(gate_recv, gate_recv_sem)
    frame_lane = lax.broadcasted_iota(jnp.int32, (frames, LANES), 1)
    for m in range(micro):
        mask, inv_rms, gate_val = masks[m], inv_all[m], gate_all[m]
        picked = jnp.dot(
            exp_all[m],
            gate_recv[...].reshape(n, LANES),
            preferred_element_type=jnp.float32,
            precision=lax.Precision.HIGHEST,
        )
        gate_grad = jnp.sum(
            jnp.where(frame_lane == slot_all[m] + m * gate_span, picked, 0.0),
            axis=1,
            keepdims=True,
        )
        cent_scale = gate_val * (1.0 - gate_val) * gate_grad
        arrived(home_ref.at[m], home_sem.at[m])
        from_blocks(home_ref.at[m])
        slot_back[...] = jnp.dot(slot_hot[m], rows_ref[...], preferred_element_type=jnp.float32)

        def scaling(c, total):
            lanes = pl.ds(pl.multiple_of(c * LANES, LANES), LANES)
            grad = gate_val * slot_back[:, lanes] + cent_scale * cent_rows[m, :, lanes].astype(
                jnp.float32
            )
            scaled = grad * gain_f[c]
            slot_back[:, lanes] = scaled
            return total + resid_ref[m, c] * scaled

        total = lax.fori_loop(0, chunks, scaling, jnp.zeros((frames, LANES), jnp.float32))
        mean = jnp.sum(total, axis=1, keepdims=True) * (1.0 / width)
        back_scale = inv_rms * inv_rms * inv_rms * mean

        def finish(c, carry):
            lanes = pl.ds(pl.multiple_of(c * LANES, LANES), LANES)
            resid_grad = (
                grad_ref[m, :, lanes].astype(jnp.float32)
                + inv_rms * slot_back[:, lanes]
                - resid_ref[m, c] * back_scale
            )
            pad_ref[c, low : low + frames, :] = slope_ref[m, c] * resid_grad
            acc = conv(c, 1, lambda first: 2 * low - first)
            out_ref[m, :, lanes] = (resid_grad + mask * acc).astype(jnp.bfloat16)
            return carry

        lax.fori_loop(0, chunks, finish, 0)

    for m in range(micro):
        departed(send_ref.at[m], send_sem.at[m])
        departed(back_ref.at[m], back_sem.at[m])
    departed(gate_send, gate_send_sem)


def block_grads(
    grads, feats, lengths, routed, slot_pos, preact, conv_k, gain, cent, weight_in, weight_out
):
    micro, frames, width = feats.shape
    n = lax.axis_size("expert")
    hidden = weight_in.shape[1]
    cap = preact.shape[1] // n
    whole_rows = 16 * LANES // math.gcd(16 * LANES, width)
    slot_cap = -(-cap // whole_rows) * whole_rows
    if slot_cap != cap:
        preact = jnp.pad(
            preact.reshape(micro, n, cap, hidden), ((0, 0), (0, 0), (0, slot_cap - cap), (0, 0))
        ).reshape(micro, n * slot_cap, hidden)
    slots = n * slot_cap
    chunks = width // LANES
    taps = conv_k.shape[0]
    block = (n, slot_cap * chunks, LANES)
    bf16, f32 = jnp.bfloat16, jnp.float32
    lengths = lengths.reshape(1, micro)
    held = (
        lengths, routed, slot_pos, conv_k, gain, cent, feats, grads, preact, weight_in, weight_out
    )
    operands = [pltpu.with_memory_space_constraint(x, pltpu.HBM) for x in held]
    in_hbm = pl.BlockSpec(memory_space=pltpu.HBM)
    dma = pltpu.SemaphoreType.DMA
    flops = micro * (4 * slots * width * hidden + 4 * frames * width * (taps + slots))
    return pl.pallas_call(
        functools.partial(kernel, "expert", n, slot_cap),
        out_shape=jax.ShapeDtypeStruct((micro, frames, width), bf16),
        in_specs=[in_hbm] * 11,
        out_specs=pl.BlockSpec(memory_space=pltpu.VMEM),
        scratch_shapes=[
            pltpu.SMEM((1, micro), jnp.int32),
            pltpu.VMEM((micro, frames), jnp.int32),
            pltpu.VMEM((micro, frames), jnp.int32),
            pltpu.VMEM((taps, width), bf16),
            pltpu.VMEM((1, width), bf16),
            pltpu.VMEM((n, width), bf16),
            pltpu.VMEM((micro, frames, width), bf16),
            pltpu.VMEM((micro, frames, width), bf16),
            pltpu.VMEM((micro, slots, hidden), bf16),
            pltpu.VMEM((width, hidden), bf16),
            pltpu.VMEM((hidden, width), bf16),
            pltpu.VMEM((chunks, taps, LANES), f32),
            pltpu.VMEM((chunks, 1, LANES), f32),
            pltpu.VMEM((micro, *block), bf16),
            pltpu.VMEM((micro, *block), bf16),
            pltpu.VMEM((micro, *block), bf16),
            pltpu.VMEM((micro, *block), bf16),
            pltpu.VMEM((n, 1, LANES), f32),
            pltpu.VMEM((n, 1, LANES), f32),
            pltpu.VMEM((slots * chunks, LANES), f32),
            pltpu.VMEM((slots, width), bf16),
            pltpu.VMEM((chunks, frames + taps, LANES), f32),
            pltpu.VMEM((micro, chunks, frames, LANES), f32),
            pltpu.VMEM((micro, chunks, frames, LANES), f32),
            pltpu.VMEM((micro, frames, width), bf16),
            pltpu.VMEM((micro, slots, hidden), f32),
            pltpu.VMEM((micro, slots, hidden), f32),
            pltpu.VMEM((frames, width), f32),
            dma((2 * micro + 9,)),
            dma((micro,)),
            dma((micro,)),
            dma((micro,)),
            dma((micro,)),
            dma,
            dma,
        ],
        compiler_params=pltpu.CompilerParams(
            collective_id=0, has_side_effects=True, vmem_limit_bytes=32 * 1024 * 1024
        ),
        cost_estimate=pl.CostEstimate(
            flops=flops, bytes_accessed=8 * 1024 * 1024, transcendentals=0
        ),
    )(*operands)


def on_device(
    feat_saved,
    out_grad,
    lengths,
    expert_ids,
    slot_ids,
    expert_preact,
    conv_weight,
    norm_gain,
    centroids,
    w_in,
    w_out,
):
    section_count = lax.axis_size("section")
    micro_count = out_grad.shape[0]
    feats, routed, slots, preact = feat_saved[0], expert_ids[0], slot_ids[0], expert_preact[0]
    fixed = (conv_weight[0], norm_gain, centroids[0], w_in[0, 0], w_out[0, 0])
    if section_count == 1:
        return block_grads(out_grad, feats, lengths, routed, slots, preact, *fixed)[None]

    section_idx = lax.axis_index("section")
    route = [(i + 1, i) for i in range(section_count - 1)]

    def one_tick(tick_idx, carry):
        incoming, grads = carry
        micro_pos = tick_idx - (section_count - 1 - section_idx)
        is_valid = jnp.logical_and(micro_pos >= 0, micro_pos < micro_count)
        micro_sel = jnp.clip(micro_pos, 0, micro_count - 1)

        def pick(array):
            return lax.dynamic_slice_in_dim(array, micro_sel, 1, 0)

        grad_in = jnp.where(section_idx == section_count - 1, pick(out_grad), incoming)
        new_grad = block_grads(
            grad_in, pick(feats), pick(lengths), pick(routed), pick(slots), pick(preact), *fixed
        )
        updated = lax.dynamic_update_slice_in_dim(grads, new_grad, micro_sel, 0)
        grads = jnp.where(is_valid, updated, grads)
        return (lax.ppermute(new_grad, "section", route), grads)

    start = (jnp.zeros((1, *out_grad.shape[1:]), jnp.bfloat16), jnp.zeros_like(out_grad))
    _, grads = lax.fori_loop(0, section_count + micro_count - 1, one_tick, start)
    return grads[None]


def solution(mesh):
    in_specs = (
        P("section", None, "expert", None),
        P(None, "expert", None),
        P(None, "expert"),
        P("section", None, "expert"),
        P("section", None, "expert"),
        P("section", None, "expert", None),
        P("section", None, None),
        P("section", None),
        P("section", None, None),
        P("section", "expert", None, None),
        P("section", "expert", None, None),
    )
    out_specs = P("section", None, "expert", None)
    return jax.shard_map(
        on_device, mesh=mesh, in_specs=in_specs, out_specs=out_specs, check_vma=False
    )
```
